128 devices in a mesh: view: 32 (over x, z, core), head: 4 (over y).
Axes of the slice: x: 4, y: 4, z: 4, core: 2. Of those that a mesh axis runs over, the one named last changes fastest.
Arguments:
- queries: bfloat16 [64, 128, 3072], P('view', None, 'head'), may hold values from -8 to 8
- keys: bfloat16 [64, 128, 3072], P('view', None, 'head'), may hold values from -8 to 8
- values: bfloat16 [64, 128, 3072], P('view', None, 'head'), may hold values from -6 to 6
- d_out: bfloat16 [64, 128, 3072], P('view', None, 'head'), may hold values from -6 to 6
- w_out: bfloat16 [3072, 3072], P('head'), may hold values from -0.109375 to 0.109375
- intersection: int32 [64, 4], replicated, may hold values from 0 to 1, as said below
Outputs:
- attended: bfloat16 [64, 128, 3072], P('view', None, 'head')
- grad_queries: bfloat16 [64, 128, 3072], P('view', None, 'head')
- grad_keys: bfloat16 [64, 128, 3072], P('view', None, 'head')
- grad_values: bfloat16 [64, 128, 3072], P('view', None, 'head')
The draws below stay inside these ranges and needn't reach their ends.
Inputs may be any that keep to these rules, and one draw needn't show every extreme that they name: intersection[v, k] is 1 when views v and v + k + 1 intersect; it is 0 wherever v + k + 1 >= 64.
All inputs are finite; a program needn't handle non-finite values.
Results may differ from the reference program's by a relative error of at most 0.02.
Values may be sent and summed in bfloat16 or wider, within the bound.
No kernel may reach another device: no remote copies, remote signals or barrier semaphores. Data moves between devices by JAX's collectives and lax.ppermute only.
A program may use at most 128 MiB of HBM per device.

```python
import jax
import jax.numpy as jnp
from jax import lax

HEADS = 32
HEAD_DIM = 96
D = 3072
TOKENS = 128
REACH = 4
VIEWS = 64


def draw_queries(key, part):
    key = jax.random.fold_in(key, 11)
    shape = (VIEWS, TOKENS, HEADS * HEAD_DIM)
    rows = jnp.clip(jax.random.normal(key, shape, jnp.float32), -4.0, 4.0)
    return rows.astype(jnp.bfloat16)


def draw_keys(key, part):
    key = jax.random.fold_in(key, 12)
    shape = (VIEWS, TOKENS, HEADS * HEAD_DIM)
    rows = jnp.clip(jax.random.normal(key, shape, jnp.float32), -4.0, 4.0)
    return rows.astype(jnp.bfloat16)


def draw_intersection(key, part):
    key = jax.random.fold_in(key, 13)
    rate_key, roll_key = jax.random.split(key)
    rates = jax.random.randint(rate_key, (VIEWS, 1), 10, 96)
    rolls = jax.random.randint(roll_key, (VIEWS, REACH), 0, 100)
    inside = jnp.arange(VIEWS)[:, None] + jnp.arange(REACH)[None, :] + 1 < VIEWS
    return jnp.where((rolls < rates) & inside, 1, 0).astype(jnp.int32)


def level_of(stream_key, extent, cuts, least, largest):
    def one(axis_at, shards_of):
        steps = jax.random.uniform(jax.random.fold_in(jax.random.fold_in(stream_key, 6), axis_at), (shards_of,), jnp.float32, least / len(cuts), largest / len(cuts))
        return jnp.repeat(jnp.exp(steps), extent[axis_at] // shards_of).reshape((-1,) + (1,) * (len(extent) - axis_at - 1))

    loudness = one(*cuts[0])
    for cut in cuts[1:]:
        loudness = loudness * one(*cut)
    return loudness


def noise(rng, extent, deviation, bound, pieces=(), held_as=jnp.bfloat16):
    loudness = level_of(rng, extent, pieces, -0.22, 0.18) if pieces else 1.0
    drawn = jax.random.normal(rng, extent, jnp.float32) * deviation * loudness
    return jnp.minimum(jnp.maximum(drawn, -bound), bound).astype(held_as)


def setup_inputs(seed: int = 0) -> dict:
    seeds = jax.random.split(jax.random.key(seed), 7)
    return {
        "queries": draw_queries(jax.random.fold_in(seeds[6], 71), 0),
        "keys": draw_keys(jax.random.fold_in(seeds[6], 71), 0),
        "values": noise(seeds[2], (VIEWS, TOKENS, D), 1.0, 6.0, ((0, 32), (2, 4))),
        "d_out": noise(seeds[3], (VIEWS, TOKENS, D), 1.0, 6.0, ((0, 32), (2, 4))),
        "w_out": noise(seeds[4], (D, D), D ** -0.5, 0.109375, ((0, 4),)),
        "intersection": draw_intersection(jax.random.fold_in(seeds[6], 71), 0),
    }


def rounded(x):
    return lax.optimization_barrier(x.astype(jnp.bfloat16)).astype(jnp.float32)


def reference(queries, keys, values, d_out, w_out, intersection):
    width = HEADS * HEAD_DIM
    span = 2 * REACH + 1
    scale = HEAD_DIM ** -0.5
    offsets = jnp.arange(-REACH, REACH + 1, dtype=jnp.int32)
    view_ids = jnp.arange(VIEWS, dtype=jnp.int32)[:, None]
    partner = view_ids + offsets[None, :]
    lower = jnp.where(offsets[None, :] > 0, view_ids, partner)
    gap = jnp.clip(jnp.abs(offsets) - 1, 0, REACH - 1).astype(jnp.int32)
    padded_intersection = jnp.pad(intersection, ((REACH, REACH), (0, 0)))
    flagged = padded_intersection[(lower + REACH).astype(jnp.int32), gap[None, :]]
    valid = (offsets[None, :] == 0) | ((flagged > 0) & (partner >= 0) & (partner < VIEWS))
    key_pad = jnp.pad(keys, ((REACH, REACH), (0, 0), (0, 0)))
    value_pad = jnp.pad(values, ((REACH, REACH), (0, 0), (0, 0)))

    def per_view(carry, inputs):
        grad_k, grad_v = carry
        query_rows, cot_rows, mask, index = inputs
        key_win = lax.dynamic_slice_in_dim(key_pad, index, span, 0)
        value_win = lax.dynamic_slice_in_dim(value_pad, index, span, 0)
        q4 = query_rows.astype(jnp.float32).reshape(TOKENS, HEADS, HEAD_DIM)
        k4 = key_win.astype(jnp.float32).reshape(span, TOKENS, HEADS, HEAD_DIM)
        v4 = value_win.astype(jnp.float32).reshape(span, TOKENS, HEADS, HEAD_DIM)
        scores = jnp.einsum("thd,wshd->htws", q4, k4) * scale
        scores = jnp.where(mask[None, None, :, None], scores, -jnp.inf)
        top = jnp.max(scores, axis=(2, 3), keepdims=True)
        lse = top + jnp.log(jnp.sum(jnp.exp(scores - top), axis=(2, 3), keepdims=True))
        weights = jnp.exp(scores - lse)
        low = rounded(weights)
        attn = jnp.einsum("htws,wshd->thd", low, v4).reshape(TOKENS, width).astype(jnp.bfloat16)
        attended = jnp.dot(attn, w_out, preferred_element_type=jnp.float32).astype(jnp.bfloat16)
        d_attn = jnp.dot(cot_rows, w_out.T, preferred_element_type=jnp.float32).astype(jnp.bfloat16)
        d4 = d_attn.astype(jnp.float32).reshape(TOKENS, HEADS, HEAD_DIM)
        a4 = attn.astype(jnp.float32).reshape(TOKENS, HEADS, HEAD_DIM)
        delta = jnp.einsum("thd,thd->ht", d4, a4)
        d_probs = jnp.einsum("thd,wshd->htws", d4, v4)
        d_scores = rounded(weights * (d_probs - delta[:, :, None, None]) * scale)
        grad_q = jnp.einsum("htws,wshd->thd", d_scores, k4).reshape(TOKENS, width).astype(jnp.bfloat16)
        part_k = jnp.einsum("htws,thd->wshd", d_scores, q4).reshape(span, TOKENS, width)
        part_v = jnp.einsum("htws,thd->wshd", low, d4).reshape(span, TOKENS, width)
        grad_k = lax.dynamic_update_slice_in_dim(grad_k, lax.dynamic_slice_in_dim(grad_k, index, span, 0) + part_k, index, 0)
        grad_v = lax.dynamic_update_slice_in_dim(grad_v, lax.dynamic_slice_in_dim(grad_v, index, span, 0) + part_v, index, 0)
        return (grad_k, grad_v), (attended, grad_q)

    start = (jnp.zeros((VIEWS + 2 * REACH, TOKENS, width), jnp.float32), jnp.zeros((VIEWS + 2 * REACH, TOKENS, width), jnp.float32))
    (grad_k, grad_v), (attended, grad_q) = lax.scan(per_view, start, (queries, d_out, valid, jnp.arange(VIEWS, dtype=jnp.int32)))
    grad_keys = grad_k[REACH:REACH + VIEWS].astype(jnp.bfloat16)
    grad_values = grad_v[REACH:REACH + VIEWS].astype(jnp.bfloat16)
    return (attended, grad_q, grad_keys, grad_values)
```

```python
from functools import partial

import jax
import jax.numpy as jnp
from jax import lax
from jax.experimental import pallas as pl
from jax.experimental.pallas import tpu as pltpu
from jax.sharding import PartitionSpec as P

HEAD_DIM = 96
REACH = 4
GROUP = 4
COLS = GROUP * HEAD_DIM
BLOCKS = 5
SCALE = HEAD_DIM ** (-0.5)
LOG2E = 1.4426950408889634
FAR = -1e30
VMEM_LIMIT = 40 * 1024 * 1024
BF16 = jnp.bfloat16
F32 = jnp.float32


def send(array, axis, pairs):
    return lax.ppermute(array, axis, pairs)


def to_sibling(array, count):
    return send(array, "view", [(i, i ^ 1) for i in range(count)])


def from_chip_a(array, count):
    pairs = [(i, i + 2) if i % 2 else (i, i - 2) for i in range(count)]
    return send(array, "view", [(s, t) for s, t in pairs if 0 <= t < count])


def from_chip_b(array, count):
    pairs = [(i, i - 2) if i % 2 else (i, i + 2) for i in range(count)]
    return send(array, "view", [(s, t) for s, t in pairs if 0 <= t < count])


def window(array, count):
    far_a = from_chip_a(array, count)
    far_b = from_chip_b(array, count)
    near = to_sibling(array, count)
    return (array, near, far_a, to_sibling(far_a, count), far_b)


def head_span(i):
    lo = i * HEAD_DIM // 128 * 128
    hi = -(-(i + 1) * HEAD_DIM // 128) * 128
    return lo, hi


def head_mask(i, rows, lo, hi):
    lane = lax.broadcasted_iota(jnp.int32, (rows, hi - lo), 1) + lo
    return (lane >= i * HEAD_DIM) & (lane < (i + 1) * HEAD_DIM)


def head_rows(ref, i, lo, hi):
    rows = ref.shape[0]
    mask = head_mask(i, 1, lo, hi).astype(F32).astype(BF16)
    return ref[:, lo:hi] * jnp.broadcast_to(mask, (rows, hi - lo))


def dot_nt(a, b):
    return lax.dot_general(a, b, (((1,), (1,)), ((), ())), preferred_element_type=F32)


def dot_nn(a, b):
    return jnp.dot(a, b, preferred_element_type=F32)


def put_lane(tile, lane, column):
    at = lax.broadcasted_iota(jnp.int32, tile.shape, 1)
    return jnp.where(at == lane, column, tile)


def add_head(total, i, lo, hi, part):
    part = jnp.where(head_mask(i, part.shape[0], lo, hi), part, 0.0)
    total[:, lo:hi] += part


def forward_kernel(q_ref, *refs):
    k_refs, v_refs = refs[:BLOCKS], refs[BLOCKS : 2 * BLOCKS]
    bias_ref, attn_ref, p_ref, stat_ref, s_ref, total = refs[2 * BLOCKS :]
    rows = q_ref.shape[0]
    total[...] = jnp.zeros_like(total)
    stat = jnp.zeros((rows, 128), F32)
    for i in range(GROUP):
        lo, hi = head_span(i)
        query = head_rows(q_ref, i, lo, hi)
        top = jnp.full((rows, 1), FAR, F32)
        for b in range(BLOCKS):
            at = slice(b * rows, (b + 1) * rows)
            scores = dot_nt(query, k_refs[b][:, lo:hi]) * (SCALE * LOG2E)
            half = rows // 2
            scores = jnp.concatenate(
                [scores[:half] + bias_ref[0:1, at], scores[half:] + bias_ref[1:2, at]], axis=0
            )
            s_ref[i % 2, :, at] = scores
            top = jnp.maximum(top, jnp.max(scores, axis=1, keepdims=True))
        norm = jnp.zeros((rows, 1), F32)
        out = jnp.zeros((rows, hi - lo), F32)
        for b in range(BLOCKS):
            at = slice(b * rows, (b + 1) * rows)
            weights = jnp.exp2(s_ref[i % 2, :, at] - top)
            norm += jnp.sum(weights, axis=1, keepdims=True)
            low = weights.astype(BF16)
            p_ref[i, :, at] = low
            out += dot_nn(low, v_refs[b][:, lo:hi])
        add_head(total, i, lo, hi, out / norm)
        stat = put_lane(stat, i, top + jnp.log2(norm))
        stat = put_lane(stat, GROUP + i, SCALE / norm)
    attn_ref[...] = total[...].astype(BF16)
    stat_ref[0] = stat


def forward(q, k, v, bias):
    rows, width = q.shape
    groups = width // COLS
    block = pl.BlockSpec((rows, COLS), lambda g: (0, g))
    return pl.pallas_call(
        forward_kernel,
        grid=(groups,),
        in_specs=[block] * (1 + 2 * BLOCKS) + [pl.BlockSpec(bias.shape, lambda g: (0, 0))],
        out_specs=[
            block,
            pl.BlockSpec((GROUP, rows, BLOCKS * rows), lambda g: (g, 0, 0)),
            pl.BlockSpec((1, rows, 128), lambda g: (g, 0, 0)),
        ],
        out_shape=[
            jax.ShapeDtypeStruct((rows, width), BF16),
            jax.ShapeDtypeStruct((groups * GROUP, rows, BLOCKS * rows), BF16),
            jax.ShapeDtypeStruct((groups, rows, 128), F32),
        ],
        scratch_shapes=[
            pltpu.VMEM((2, rows, BLOCKS * rows), F32),
            pltpu.VMEM((rows, COLS), F32),
        ],
        compiler_params=pltpu.CompilerParams(vmem_limit_bytes=VMEM_LIMIT),
        cost_estimate=pl.CostEstimate(
            flops=4 * rows * rows * BLOCKS * width, bytes_accessed=10_000_000, transcendentals=0
        ),
        name="forward",
    )(q, *k, *v, bias)


def d_attn_kernel(order_ref, d0, d1, d2, d3, w_ref, out_ref, total):
    step = pl.program_id(0)
    for n, d_ref in enumerate((d0, d1, d2, d3)):

        @pl.when(step == n)
        def _():
            part = dot_nt(d_ref[...], w_ref[...])
            if n == 0:
                total[...] = part
            else:
                total[...] += part

    @pl.when(step == 3)
    def _():
        out_ref[...] = total[...].astype(BF16)


def attn_cotangent(order, parts, w_out):
    rows, width = parts[0].shape
    whole = pl.BlockSpec((rows, width), lambda s, order: (0, 0))
    return pl.pallas_call(
        d_attn_kernel,
        grid_spec=pltpu.PrefetchScalarGridSpec(
            num_scalar_prefetch=1,
            grid=(4,),
            in_specs=[whole] * 4 + [pl.BlockSpec((width, width), lambda s, order: (0, order[s]))],
            out_specs=whole,
            scratch_shapes=[pltpu.VMEM((rows, width), F32)],
        ),
        out_shape=jax.ShapeDtypeStruct((rows, width), BF16),
        compiler_params=pltpu.CompilerParams(vmem_limit_bytes=VMEM_LIMIT),
        cost_estimate=pl.CostEstimate(
            flops=8 * rows * width * width, bytes_accessed=7_000_000, transcendentals=0
        ),
        name="attn_cotangent",
    )(order, *parts, w_out)


def project_kernel(order_ref, attn_ref, d_ref, stat_ref, w_ref, o1, o2, o3, own, stat_out, rows_out):
    step = pl.program_id(0)

    @pl.when(step == 0)
    def _():
        product = attn_ref[...].astype(F32) * d_ref[...].astype(F32)
        for g in range(stat_ref.shape[0]):
            stat = stat_ref[g]
            for i in range(GROUP):
                lo, hi = head_span(i)
                mine = jnp.where(
                    head_mask(i, product.shape[0], lo, hi),
                    product[:, g * COLS + lo : g * COLS + hi],
                    0.0,
                )
                stat = put_lane(stat, 2 * GROUP + i, jnp.sum(mine, axis=1, keepdims=True))
            stat_out[g] = stat
            rows_out[g] = stat.T[: 4 * GROUP]

    for n, out_ref in enumerate((o1, o2, o3, own)):

        @pl.when(step == n)
        def _():
            out_ref[...] = dot_nn(attn_ref[...], w_ref[...]).astype(out_ref.dtype)


def project(order, attn, d_attn, stat, w_out):
    rows, width = attn.shape
    groups = stat.shape[0]
    whole = pl.BlockSpec((rows, width), lambda s, order: (0, 0))
    stats = pl.BlockSpec((groups, rows, 128), lambda s, order: (0, 0, 0))
    return pl.pallas_call(
        project_kernel,
        grid_spec=pltpu.PrefetchScalarGridSpec(
            num_scalar_prefetch=1,
            grid=(4,),
            in_specs=[
                whole,
                whole,
                stats,
                pl.BlockSpec((width, width), lambda s, order: (0, order[s])),
            ],
            out_specs=[whole] * 4
            + [stats, pl.BlockSpec((groups, 4 * GROUP, rows), lambda s, order: (0, 0, 0))],
        ),
        out_shape=[jax.ShapeDtypeStruct((rows, width), BF16)] * 3
        + [
            jax.ShapeDtypeStruct((rows, width), F32),
            jax.ShapeDtypeStruct((groups, rows, 128), F32),
            jax.ShapeDtypeStruct((groups, 4 * GROUP, rows), F32),
        ],
        compiler_params=pltpu.CompilerParams(vmem_limit_bytes=VMEM_LIMIT),
        cost_estimate=pl.CostEstimate(
            flops=8 * rows * width * width, bytes_accessed=8_000_000, transcendentals=0
        ),
        name="project",
    )(order, attn, d_attn, stat, w_out)


def query_grad_kernel(p_ref, d_ref, stat_ref, *refs):
    k_refs, v_refs = refs[:BLOCKS], refs[BLOCKS : 2 * BLOCKS]
    out_ref, total = refs[2 * BLOCKS :]
    rows = d_ref.shape[0]
    total[...] = jnp.zeros_like(total)
    for i in range(GROUP):
        lo, hi = head_span(i)
        cot = head_rows(d_ref, i, lo, hi)
        delta = stat_ref[0, :, 2 * GROUP + i : 2 * GROUP + i + 1]
        scale = stat_ref[0, :, GROUP + i : GROUP + i + 1]
        grad = jnp.zeros((rows, hi - lo), F32)
        for b in range(BLOCKS):
            at = slice(b * rows, (b + 1) * rows)
            d_probs = dot_nt(cot, v_refs[b][:, lo:hi])
            d_scores = (p_ref[i, :, at].astype(F32) * (d_probs - delta)).astype(BF16)
            grad += dot_nn(d_scores, k_refs[b][:, lo:hi])
        add_head(total, i, lo, hi, grad * scale)
    out_ref[...] = total[...].astype(BF16)


def query_grad(p, d_attn, stat, k, v):
    rows, width = d_attn.shape
    groups = width // COLS
    block = pl.BlockSpec((rows, COLS), lambda g: (0, g))
    return pl.pallas_call(
        query_grad_kernel,
        grid=(groups,),
        in_specs=[
            pl.BlockSpec((GROUP, rows, BLOCKS * rows), lambda g: (g, 0, 0)),
            block,
            pl.BlockSpec((1, rows, 128), lambda g: (g, 0, 0)),
        ]
        + [block] * (2 * BLOCKS),
        out_specs=block,
        out_shape=jax.ShapeDtypeStruct((rows, width), BF16),
        scratch_shapes=[pltpu.VMEM((rows, COLS), F32)],
        compiler_params=pltpu.CompilerParams(vmem_limit_bytes=VMEM_LIMIT),
        cost_estimate=pl.CostEstimate(
            flops=4 * rows * rows * BLOCKS * width, bytes_accessed=10_000_000, transcendentals=0
        ),
        name="query_grad",
    )(p, d_attn, stat, *k, *v)


def key_grad_kernel(k_ref, v_ref, bias_ref, *refs):
    q_refs, d_refs, s_refs = (refs[n * BLOCKS : (n + 1) * BLOCKS] for n in range(3))
    gk_ref, gv_ref, total_k, total_v = refs[3 * BLOCKS :]
    rows = k_ref.shape[0]
    half = rows // 2
    total_k[...] = jnp.zeros_like(total_k)
    total_v[...] = jnp.zeros_like(total_v)
    for i in range(GROUP):
        lo, hi = head_span(i)
        key = head_rows(k_ref, i, lo, hi)
        value = head_rows(v_ref, i, lo, hi)
        grad_k = jnp.zeros((rows, hi - lo), F32)
        grad_v = jnp.zeros((rows, hi - lo), F32)
        for b in range(BLOCKS):
            at = slice(b * rows, (b + 1) * rows)
            query = q_refs[b][:, lo:hi]
            cot = d_refs[b][:, lo:hi]
            shift = bias_ref[:, at] - s_refs[b][0, i : i + 1]
            delta = s_refs[b][0, 2 * GROUP + i : 2 * GROUP + i + 1]
            scores = dot_nt(key, query) * (SCALE * LOG2E)
            weights = jnp.exp2(
                jnp.concatenate([scores[:half] + shift[0:1], scores[half:] + shift[1:2]], axis=0)
            )
            grad_v += dot_nn(weights.astype(BF16), cot)
            d_probs = dot_nt(value, cot)
            grad_k += dot_nn((weights * (d_probs - delta)).astype(BF16), query)
        add_head(total_k, i, lo, hi, grad_k * SCALE)
        add_head(total_v, i, lo, hi, grad_v)
    gk_ref[...] = total_k[...].astype(BF16)
    gv_ref[...] = total_v[...].astype(BF16)


def key_grad(k, v, bias, q, d, stats):
    rows, width = k.shape
    groups = width // COLS
    block = pl.BlockSpec((rows, COLS), lambda g: (0, g))
    return pl.pallas_call(
        key_grad_kernel,
        grid=(groups,),
        in_specs=[block, block, pl.BlockSpec(bias.shape, lambda g: (0, 0))]
        + [block] * (2 * BLOCKS)
        + [pl.BlockSpec((1, 4 * GROUP, rows), lambda g: (g, 0, 0))] * BLOCKS,
        out_specs=[block, block],
        out_shape=[jax.ShapeDtypeStruct((rows, width), BF16)] * 2,
        scratch_shapes=[pltpu.VMEM((rows, COLS), F32)] * 2,
        compiler_params=pltpu.CompilerParams(vmem_limit_bytes=VMEM_LIMIT),
        cost_estimate=pl.CostEstimate(
            flops=8 * rows * rows * BLOCKS * width, bytes_accessed=6_000_000, transcendentals=0
        ),
        name="key_grad",
    )(k, v, bias, *q, *d, *stats)


def window_bias(intersection, base, odd, length):
    padded = jnp.pad(intersection, ((REACH, REACH), (0, 0)))
    near = lax.dynamic_slice(padded, (base, 0), (2 * REACH + 2, REACH))
    table = []
    for local in range(2):
        for other in range(2 * REACH + 2):
            gap = other - REACH - local
            if gap == 0:
                table.append(jnp.ones((), jnp.int32))
            elif abs(gap) > REACH:
                table.append(jnp.zeros((), jnp.int32))
            else:
                table.append(near[min(other, local + REACH), abs(gap) - 1])
    flags = jnp.stack(table).reshape(2, BLOCKS, 2)
    even_order = (2, 3, 4, 1, 0)
    ordered = jnp.where(
        odd,
        jnp.stack([flags[:, 4 - b] for b in even_order], 1),
        jnp.stack([flags[:, b] for b in even_order], 1),
    ).reshape(2, 2 * BLOCKS)
    return jnp.repeat(jnp.where(ordered > 0, 0.0, FAR).astype(F32), length, axis=1)


def body(queries, keys, values, d_out, w_out, intersection):
    count, length, width = queries.shape
    devices = lax.axis_size("view")
    groups = lax.axis_size("head")
    here = lax.axis_index("view")
    mine = lax.axis_index("head")
    q, k, v, d = (a.reshape(count * length, width) for a in (queries, keys, values, d_out))

    def from_group(array, by):
        return send(array, "head", [(i, (i - by) % groups) for i in range(groups)])

    k_win = window(k, devices)
    d_parts = [d] + [from_group(d, by) for by in (1, 3, 2)]
    v_win = window(v, devices)
    q_win = window(q, devices)
    bias = window_bias(intersection, here * count, here % 2 == 1, length)
    order = jnp.stack([(mine + by) % groups for by in (0, 1, 3, 2)]).astype(jnp.int32)
    d_attn = attn_cotangent(order, d_parts, w_out)
    d_win = window(d_attn, devices)
    attn, p, stat = forward(q, k_win, v_win, bias)
    out_order = jnp.stack([(mine + by) % groups for by in (1, 3, 2, 0)]).astype(jnp.int32)
    to_next, to_last, to_far, own, stat, stat_rows = project(out_order, attn, d_attn, stat, w_out)
    stats = window(stat_rows, devices)
    gained = [from_group(part, by) for part, by in ((to_next, 3), (to_last, 1), (to_far, 2))]
    grad_q = query_grad(p, d_attn, stat, k_win, v_win)
    grad_k, grad_v = key_grad(k, v, bias, q_win, d_win, stats)
    attended = (own + sum(part.astype(F32) for part in gained)).astype(BF16)
    shape = (count, length, width)
    return tuple(a.reshape(shape) for a in (attended, grad_q, grad_k, grad_v))


def solution(mesh):
    columns = P("view", None, "head")
    return jax.shard_map(
        body,
        mesh=mesh,
        in_specs=(columns, columns, columns, columns, P("head", None), P()),
        out_specs=(columns, columns, columns, columns),
        check_vma=False,
    )
```

```python
from functools import partial

import jax
import jax.numpy as jnp
from jax import lax
from jax.experimental import pallas as pl
from jax.experimental.pallas import tpu as pltpu
from jax.sharding import PartitionSpec as P

HEAD_DIM = 96
REACH = 4
GROUP = 4
COLS = GROUP * HEAD_DIM
BLOCKS = 5
SCALE = HEAD_DIM ** (-0.5)
LOG2E = 1.4426950408889634
FAR = -1e30
VMEM_LIMIT = 18 * 1024 * 1024
SMALL_LIMIT = 1024 * 1024
BF16 = jnp.bfloat16
F32 = jnp.float32
SCALARS = pl.BlockSpec(memory_space=pltpu.SMEM)
COST = pl.CostEstimate(flops=1000, bytes_accessed=1000, transcendentals=0)


def declared(megabytes):
    return pl.CostEstimate(flops=megabytes * 300_000_000, bytes_accessed=1000, transcendentals=0)


C0, C1, C2, C3 = 20, 1, 1, 1
ORDER = pl.BlockSpec(memory_space=pl.ANY)
STAT_ROWS = 16


def send(array, axis, pairs):
    return lax.ppermute(array, axis, pairs)


def to_sibling(array, count):
    return send(array, "view", [(i, i ^ 1) for i in range(count)])


def from_chip_a(array, count):
    return send(array, "view", [(i, (i + (2 if i % 2 else -2)) % count) for i in range(count)])


def from_chip_b(array, count):
    return send(array, "view", [(i, (i + (-2 if i % 2 else 2)) % count) for i in range(count)])


def in_hbm(array):
    return pltpu.with_memory_space_constraint(array, pltpu.HBM)


def in_vmem(arrays):
    return [pltpu.with_memory_space_constraint(a, pltpu.VMEM) for a in arrays]


def head_span(i):
    lo = i * HEAD_DIM // 128 * 128
    hi = -(-(i + 1) * HEAD_DIM // 128) * 128
    return lo, hi


def head_mask(i, rows, lo, hi):
    lane = lax.broadcasted_iota(jnp.int32, (rows, hi - lo), 1) + lo
    return (lane >= i * HEAD_DIM) & (lane < (i + 1) * HEAD_DIM)


def head_rows(ref, i, lo, hi):
    rows = ref.shape[0]
    mask = head_mask(i, 1, lo, hi).astype(F32).astype(BF16)
    return ref[:, lo:hi] * jnp.broadcast_to(mask, (rows, hi - lo))


def dot_nt(a, b):
    return lax.dot_general(a, b, (((1,), (1,)), ((), ())), preferred_element_type=F32)


def dot_nn(a, b):
    return jnp.dot(a, b, preferred_element_type=F32)


def fill_bias(linked_ref, bias_ref):
    here = lax.axis_index("view")
    base, sign = 2 * here, 1 - 2 * (here % 2)
    views = linked_ref.shape[1]
    lane = lax.broadcasted_iota(jnp.int32, (1, bias_ref.shape[1] // BLOCKS), 1)
    half = bias_ref.shape[1] // BLOCKS // 2
    for local in range(2):
        for b, offset in enumerate((0, 2, 4, -2, -4)):
            shifts = []
            for other in range(2):
                gap = sign * offset + other - local
                lower = base + local + jnp.minimum(gap, 0)
                size = jnp.abs(gap)
                row = jnp.clip(lower, 0, views - 1)
                column = jnp.clip(size - 1, 0, REACH - 1)
                linked = (linked_ref[column, row] > 0) & (lower >= 0) & (size <= REACH)
                shifts.append(jnp.where(linked | (size == 0), 0.0, FAR).astype(F32))
            at = slice(2 * b * half, 2 * (b + 1) * half)
            bias_ref[local : local + 1, at] = jnp.where(lane < half, shifts[0], shifts[1])


def put_lane(tile, lane, column):
    at = lax.broadcasted_iota(jnp.int32, tile.shape, 1)
    return jnp.where(at == lane, column, tile)


def add_head(total, i, lo, hi, part):
    part = jnp.where(head_mask(i, part.shape[0], lo, hi), part, 0.0)
    total[:, lo:hi] += part


def forward_kernel(linked_ref, after_a, after_b, q_ref, *refs):
    k_refs, v_refs = refs[:BLOCKS], refs[BLOCKS : 2 * BLOCKS]
    attn_ref, p_ref, stat_ref, s_ref, total, bias_ref = refs[2 * BLOCKS :]
    rows = q_ref.shape[0]

    @pl.when(pl.program_id(0) == 0)
    def _():
        fill_bias(linked_ref, bias_ref)

    total[...] = jnp.zeros_like(total)
    stat = jnp.zeros((rows, 128), F32)
    for i in range(GROUP):
        lo, hi = head_span(i)
        query = head_rows(q_ref, i, lo, hi)
        top = jnp.full((rows, 1), FAR, F32)
        for b in range(BLOCKS):
            at = slice(b * rows, (b + 1) * rows)
            scores = dot_nt(query, k_refs[b][:, lo:hi]) * (SCALE * LOG2E)
            half = rows // 2
            scores = jnp.concatenate(
                [scores[:half] + bias_ref[0:1, at], scores[half:] + bias_ref[1:2, at]], axis=0
            )
            s_ref[i % 2, :, at] = scores
            top = jnp.maximum(top, jnp.max(scores, axis=1, keepdims=True))
        norm = jnp.zeros((rows, 1), F32)
        out = jnp.zeros((rows, hi - lo), F32)
        for b in range(BLOCKS):
            at = slice(b * rows, (b + 1) * rows)
            weights = jnp.exp2(s_ref[i % 2, :, at] - top)
            norm += jnp.sum(weights, axis=1, keepdims=True)
            low = weights.astype(BF16)
            p_ref[i, :, at] = low
            out += dot_nn(low, v_refs[b][:, lo:hi])
        add_head(total, i, lo, hi, out / norm)
        stat = put_lane(stat, i, top + jnp.log2(norm))
        stat = put_lane(stat, GROUP + i, SCALE / norm)
    attn_ref[...] = total[...].astype(BF16)
    stat_ref[0] = stat


def rows_at(n, rows):
    return pl.BlockSpec((rows, COLS), lambda g: (n, g))


def forward(linked, after, q, k, v, windows):
    rows, width = q.shape
    groups = width // COLS
    block = pl.BlockSpec((rows, COLS), lambda g: (0, g))
    k_specs, v_specs = ([block] + [rows_at(n, rows) for w in windows] for n in (0, 1))
    windows = in_vmem(windows)
    return pl.pallas_call(
        forward_kernel,
        grid=(groups,),
        in_specs=[SCALARS, ORDER, ORDER, block] + k_specs + v_specs,
        out_specs=[
            block,
            pl.BlockSpec((GROUP, rows, BLOCKS * rows), lambda g: (g, 0, 0)),
            pl.BlockSpec((1, rows, 128), lambda g: (g, 0, 0)),
        ],
        out_shape=[
            jax.ShapeDtypeStruct((rows, width), BF16),
            jax.ShapeDtypeStruct((groups * GROUP, rows, BLOCKS * rows), BF16),
            jax.ShapeDtypeStruct((groups, rows, 128), F32),
        ],
        scratch_shapes=[
            pltpu.VMEM((2, rows, BLOCKS * rows), F32),
            pltpu.VMEM((rows, COLS), F32),
            pltpu.VMEM((2, BLOCKS * rows), F32),
        ],
        compiler_params=pltpu.CompilerParams(vmem_limit_bytes=VMEM_LIMIT),
        cost_estimate=COST,
        name="forward",
    )(linked, *after, in_hbm(q), in_hbm(k), *windows, in_hbm(v), *windows)


def fetch_columns(w_ref, held, sems, hops):
    width = held.shape[2]
    mine = lax.axis_index("head")
    copies = []
    for n, by in enumerate(hops):
        at = pl.multiple_of((mine + by) % len(hops) * width, width)
        copies.append(pltpu.make_async_copy(w_ref.at[:, pl.ds(at, width)], held.at[n], sems.at[n]))
    for copy in copies:
        copy.start()
    return copies


def d_attn_kernel(d0, d1, d2, d3, w_ref, out_ref, held, sems):
    copies = fetch_columns(w_ref, held, sems, (0, 1, 3, 2))
    total = 0.0
    for n, d_ref in enumerate((d0, d1, d2, d3)):
        copies[n].wait()
        total += dot_nt(d_ref[...], held[n])
    out_ref[...] = total.astype(BF16)


def attn_cotangent(parts, w_out):
    rows, width = parts[0].shape
    whole = pl.BlockSpec((rows, width), lambda: (0, 0))
    return pl.pallas_call(
        d_attn_kernel,
        in_specs=[whole] * 4 + [ORDER],
        out_specs=whole,
        scratch_shapes=[pltpu.VMEM((4, width, width), BF16), pltpu.SemaphoreType.DMA((4,))],
        out_shape=jax.ShapeDtypeStruct((rows, width), BF16),
        compiler_params=pltpu.CompilerParams(vmem_limit_bytes=VMEM_LIMIT),
        cost_estimate=declared(C0),
        name="attn_cotangent",
    )(in_hbm(parts[0]), *in_vmem(parts[1:]), in_hbm(w_out))


def project_kernel(attn_ref, d_ref, stat_ref, qa_ref, qb_ref, w_ref, *refs):
    parts, stat_out, message, held, sems = refs[:4], *refs[4:]
    copies = fetch_columns(w_ref, held, sems, (1, 3, 2, 0))
    rows = attn_ref.shape[0]
    message[:rows] = d_ref[...]
    product = attn_ref[...].astype(F32) * d_ref[...].astype(F32)
    slabs = []
    for g in range(stat_ref.shape[0]):
        stat = stat_ref[g]
        travels = stat
        for i in range(GROUP):
            lo, hi = head_span(i)
            mine = jnp.where(
                head_mask(i, rows, lo, hi), product[:, g * COLS + lo : g * COLS + hi], 0.0
            )
            delta = jnp.sum(mine, axis=1, keepdims=True)
            stat = put_lane(stat, 2 * GROUP + i, delta)
            travels = put_lane(travels, GROUP + i, delta)
        stat_out[g] = stat
        slabs.append(travels.T[: 2 * GROUP])
    rest = jnp.concatenate(slabs, axis=0)
    for n in range(3):
        piece = rest.astype(BF16)
        message[rows:, n * rows : (n + 1) * rows] = piece
        rest = rest - piece.astype(F32)
    for n, out_ref in enumerate(parts):
        copies[n].wait()
        out_ref[...] = dot_nn(attn_ref[...], held[n]).astype(out_ref.dtype)


def project(attn, d_attn, stat, after, w_out):
    rows, width = attn.shape
    groups = stat.shape[0]
    whole = pl.BlockSpec((rows, width), lambda: (0, 0))
    stats = pl.BlockSpec((groups, rows, 128), lambda: (0, 0, 0))
    message = pl.BlockSpec((rows + STAT_ROWS, width), lambda: (0, 0))
    return pl.pallas_call(
        project_kernel,
        in_specs=[whole, whole, stats, ORDER, ORDER, ORDER],
        out_specs=[whole] * 4 + [stats, message],
        out_shape=[jax.ShapeDtypeStruct((rows, width), BF16)] * 3
        + [
            jax.ShapeDtypeStruct((rows, width), F32),
            jax.ShapeDtypeStruct((groups, rows, 128), F32),
            jax.ShapeDtypeStruct((rows + STAT_ROWS, width), BF16),
        ],
        scratch_shapes=[pltpu.VMEM((4, width, width), BF16), pltpu.SemaphoreType.DMA((4,))],
        compiler_params=pltpu.CompilerParams(vmem_limit_bytes=VMEM_LIMIT),
        cost_estimate=COST,
        name="project",
    )(*in_vmem((attn, d_attn, stat)), *after, in_hbm(w_out))


def query_grad_kernel(p_ref, d_ref, stat_ref, *refs):
    k_refs, v_refs = refs[:BLOCKS], refs[BLOCKS : 2 * BLOCKS]
    out_ref, total = refs[2 * BLOCKS :]
    rows = d_ref.shape[0]
    total[...] = jnp.zeros_like(total)
    for i in range(GROUP):
        lo, hi = head_span(i)
        cot = head_rows(d_ref, i, lo, hi)
        delta = stat_ref[0, :, 2 * GROUP + i : 2 * GROUP + i + 1]
        scale = stat_ref[0, :, GROUP + i : GROUP + i + 1]
        grad = jnp.zeros((rows, hi - lo), F32)
        for b in range(BLOCKS):
            at = slice(b * rows, (b + 1) * rows)
            d_probs = dot_nt(cot, v_refs[b][:, lo:hi])
            d_scores = (p_ref[i, :, at].astype(F32) * (d_probs - delta)).astype(BF16)
            grad += dot_nn(d_scores, k_refs[b][:, lo:hi])
        add_head(total, i, lo, hi, grad * scale)
    out_ref[...] = total[...].astype(BF16)


def query_grad(p, d_attn, stat, k, v, windows):
    rows, width = d_attn.shape
    groups = width // COLS
    block = pl.BlockSpec((rows, COLS), lambda g: (0, g))
    k_specs, v_specs = ([block] + [rows_at(n, rows) for w in windows] for n in (0, 1))
    windows = in_vmem(windows)
    return pl.pallas_call(
        query_grad_kernel,
        grid=(groups,),
        in_specs=[
            pl.BlockSpec((GROUP, rows, BLOCKS * rows), lambda g: (g, 0, 0)),
            block,
            pl.BlockSpec((1, rows, 128), lambda g: (g, 0, 0)),
        ]
        + k_specs
        + v_specs,
        out_specs=block,
        out_shape=jax.ShapeDtypeStruct((rows, width), BF16),
        scratch_shapes=[pltpu.VMEM((rows, COLS), F32)],
        compiler_params=pltpu.CompilerParams(vmem_limit_bytes=VMEM_LIMIT),
        cost_estimate=declared(C3),
        name="query_grad",
    )(*in_vmem((p, d_attn, stat)), in_hbm(k), *windows, in_hbm(v), *windows)


def key_grad_kernel(blocks, final, linked_ref, k_ref, v_ref, *refs):
    count = len(blocks)
    q_refs, d_refs, s_refs = (refs[n * count : (n + 1) * count] for n in range(3))
    *so_far, gk_ref, gv_ref, total_k, total_v, bias_ref = refs[3 * count :]
    rows = k_ref.shape[0]
    half = rows // 2

    @pl.when(pl.program_id(0) == 0)
    def _():
        fill_bias(linked_ref, bias_ref)

    first = pl.program_id(0) == 0
    stats = []
    for s_ref in s_refs:
        packed = s_ref[...].astype(F32)
        stat = packed[:, :rows] + packed[:, rows : 2 * rows] + packed[:, 2 * rows :]
        stats.append(jnp.where(first, stat[: 2 * GROUP], stat[2 * GROUP :]))
    for total, ref in zip((total_k, total_v), so_far if final else (None, None)):
        total[...] = jnp.zeros_like(total) if ref is None else ref[...]
    for i in range(GROUP):
        lo, hi = head_span(i)
        key = head_rows(k_ref, i, lo, hi)
        value = head_rows(v_ref, i, lo, hi)
        grad_k = jnp.zeros((rows, hi - lo), F32)
        grad_v = jnp.zeros((rows, hi - lo), F32)
        for n, b in enumerate(blocks):
            at = slice(b * rows, (b + 1) * rows)
            query = q_refs[n][:, lo:hi]
            cot = d_refs[n][:, lo:hi]
            shift = bias_ref[:, at] - stats[n][i : i + 1]
            delta = stats[n][GROUP + i : GROUP + i + 1]
            scores = dot_nt(key, query) * (SCALE * LOG2E)
            weights = jnp.exp2(
                jnp.concatenate([scores[:half] + shift[0:1], scores[half:] + shift[1:2]], axis=0)
            )
            grad_v += dot_nn(weights.astype(BF16), cot)
            d_probs = dot_nt(value, cot)
            grad_k += dot_nn((weights * (d_probs - delta)).astype(BF16), query)
        add_head(total_k, i, lo, hi, grad_k)
        add_head(total_v, i, lo, hi, grad_v)
    gk_ref[...] = (total_k[...] * SCALE if final else total_k[...]).astype(gk_ref.dtype)
    gv_ref[...] = total_v[...].astype(gv_ref.dtype)


def key_grad(blocks, linked, k, v, q, q_rows, messages, so_far=(), after=()):
    rows, width = k.shape
    groups = width // COLS
    block = pl.BlockSpec((rows, COLS), lambda g: (0, g))
    stats = pl.BlockSpec((STAT_ROWS, width), lambda g: (rows // STAT_ROWS, 0))
    return pl.pallas_call(
        partial(key_grad_kernel, blocks, bool(so_far)),
        grid=(groups,),
        in_specs=[SCALARS, block, block]
        + [rows_at(n, rows) for n in q_rows]
        + [block] * len(blocks)
        + [stats] * len(blocks)
        + [block] * len(so_far)
        + [ORDER] * len(after),
        out_specs=[block, block],
        out_shape=[jax.ShapeDtypeStruct((rows, width), BF16 if so_far else F32)] * 2,
        scratch_shapes=[pltpu.VMEM((rows, COLS), F32)] * 2 + [pltpu.VMEM((2, BLOCKS * rows), F32)],
        compiler_params=pltpu.CompilerParams(vmem_limit_bytes=VMEM_LIMIT),
        cost_estimate=declared(C1) if so_far else COST,
        name="key_grad_far" if so_far else "key_grad_near",
    )(
        linked,
        in_hbm(k),
        in_hbm(v),
        *([in_hbm(q[0])] if not so_far else in_vmem(q[:1])),
        *in_vmem((*q[1:], *messages, *messages, *so_far)),
        *after,
    )


def gate_kernel(*refs):
    pass


def gate(arrays, after):
    return pl.pallas_call(
        gate_kernel,
        in_specs=[ORDER] * (len(arrays) + len(after)),
        out_specs=[ORDER] * len(arrays),
        out_shape=[jax.ShapeDtypeStruct(a.shape, a.dtype) for a in arrays],
        input_output_aliases={n: n for n in range(len(arrays))},
        compiler_params=pltpu.CompilerParams(vmem_limit_bytes=SMALL_LIMIT),
        cost_estimate=COST,
        name="gate",
    )(*in_vmem(arrays), *after)


def add_kernel(after_ref, own, a, b, c, out_ref):
    total = own[...] + a[...].astype(F32) + b[...].astype(F32) + c[...].astype(F32)
    out_ref[...] = total.astype(BF16)


def add_parts(after, own, parts):
    rows, width = own.shape
    block = pl.BlockSpec((rows, width), lambda: (0, 0))
    return pl.pallas_call(
        add_kernel,
        in_specs=[ORDER] + [block] * 4,
        out_specs=block,
        out_shape=jax.ShapeDtypeStruct((rows, width), BF16),
        compiler_params=pltpu.CompilerParams(vmem_limit_bytes=VMEM_LIMIT),
        cost_estimate=declared(C2),
        name="add_parts",
    )(after, *in_vmem((own, *parts)))


def corner_kernel(*refs):
    refs[-1][...] = jnp.zeros_like(refs[-1])


def corner(array, devices):
    shape = (16, 128)
    tile = pl.pallas_call(
        corner_kernel,
        in_specs=[ORDER],
        out_specs=pl.BlockSpec(shape, lambda: (0, 0)),
        out_shape=jax.ShapeDtypeStruct(shape, BF16),
        compiler_params=pltpu.CompilerParams(vmem_limit_bytes=SMALL_LIMIT),
        cost_estimate=COST,
        name="corner",
    )(array)
    return to_sibling(tile, devices)


def pack_kernel(k_ref, v_ref, out_ref):
    rows = k_ref.shape[0]
    out_ref[:rows] = k_ref[...]
    out_ref[rows:] = v_ref[...]


def pack(k, v):
    rows, width = k.shape
    return pl.pallas_call(
        pack_kernel,
        out_shape=jax.ShapeDtypeStruct((2 * rows, width), BF16),
        compiler_params=pltpu.CompilerParams(vmem_limit_bytes=VMEM_LIMIT),
        cost_estimate=COST,
        name="pack",
    )(in_hbm(k), in_hbm(v))


def body(queries, keys, values, d_out, w_out, intersection):
    count, length, width = queries.shape
    devices = lax.axis_size("view")
    groups = lax.axis_size("head")
    q, k, v, d = (a.reshape(count * length, width) for a in (queries, keys, values, d_out))
    linked = intersection.T

    def from_group(array, by):
        return send(array, "head", [(i, (i - by) % groups) for i in range(groups)])

    gathered = [from_group(d, by) for by in (1, 3, 2)]
    kv = pack(k, v)
    kv_a, kv_b = from_chip_a(kv, devices), from_chip_b(kv, devices)
    near = to_sibling(kv, devices)
    windows = (near, kv_a, to_sibling(kv_a, devices), kv_b)
    q_a, q_b = from_chip_a(q, devices), from_chip_b(q, devices)
    d_attn = attn_cotangent([d] + gathered, w_out)
    attn, p, stat = forward(linked, (d_attn, corner(kv_b, devices)), q, k, v, windows)
    to_next, to_last, to_far, own, stat, message = project(attn, d_attn, stat, (q_a, q_b), w_out)
    d_a, d_b = from_chip_a(message, devices), from_chip_b(message, devices)
    gained = [from_group(part, by) for part, by in ((to_next, 3), (to_last, 1), (to_far, 2))]
    grad_q = query_grad(p, d_attn, stat, k, v, windows)
    messages = (message, to_sibling(message, devices))
    q_far = (q_a, to_sibling(q_a, devices), q_b)
    part = key_grad(
        (0, 1), linked, k, v, (q, to_sibling(q, devices)), (0, 0), messages, after=q_far[1:2]
    )
    d_a, d_b = gate((d_a, d_b), (in_hbm(grad_q), part[0]))
    messages = (d_a, to_sibling(d_a, devices), d_b)
    grad_k, grad_v = key_grad((2, 3, 4), linked, k, v, q_far, (0, 0, 0), messages, part)
    attended = add_parts(message, own, gained)
    shape = (count, length, width)
    return tuple(a.reshape(shape) for a in (attended, grad_q, grad_k, grad_v))


def solution(mesh):
    columns = P("view", None, "head")
    return jax.shard_map(
        body,
        mesh=mesh,
        in_specs=(columns, columns, columns, columns, P("head", None), P()),
        out_specs=(columns, columns, columns, columns),
        check_vma=False,
    )
```

```python
from functools import partial

import jax
import jax.numpy as jnp
from jax import lax
from jax.experimental import pallas as pl
from jax.experimental.pallas import tpu as pltpu
from jax.sharding import PartitionSpec as P

HEAD_DIM = 96
REACH = 4
GROUP = 4
COLS = GROUP * HEAD_DIM
BLOCKS = 5
SCALE = HEAD_DIM ** (-0.5)
LOG2E = 1.4426950408889634
FAR = -1e30
VMEM_LIMIT = 18 * 1024 * 1024
SMALL_LIMIT = 1024 * 1024
BF16 = jnp.bfloat16
F32 = jnp.float32
SCALARS = pl.BlockSpec(memory_space=pltpu.SMEM)
COST = pl.CostEstimate(flops=1000, bytes_accessed=1000, transcendentals=0)


def declared(megabytes):
    return pl.CostEstimate(flops=megabytes * 300_000_000, bytes_accessed=1000, transcendentals=0)


C0, C1, C2, C3 = 20, 1, 30, 1
ORDER = pl.BlockSpec(memory_space=pl.ANY)
HELD = pl.BlockSpec(memory_space=pltpu.VMEM)
STAT_ROWS = 16


def send(array, axis, pairs):
    return lax.ppermute(array, axis, pairs)


def to_sibling(array, count):
    return send(array, "view", [(i, i ^ 1) for i in range(count)])


def from_chip_a(array, count):
    return send(array, "view", [(i, (i + (2 if i % 2 else -2)) % count) for i in range(count)])


def from_chip_b(array, count):
    return send(array, "view", [(i, (i + (-2 if i % 2 else 2)) % count) for i in range(count)])


def in_hbm(array):
    return pltpu.with_memory_space_constraint(array, pltpu.HBM)


def in_vmem(arrays):
    return [pltpu.with_memory_space_constraint(a, pltpu.VMEM) for a in arrays]


def head_span(h):
    lo = h * HEAD_DIM // 128 * 128
    hi = -(-(h + 1) * HEAD_DIM // 128) * 128
    return lo, hi


def head_mask(i, rows, lo, hi):
    lane = lax.broadcasted_iota(jnp.int32, (rows, hi - lo), 1) + lo
    return (lane >= i * HEAD_DIM) & (lane < (i + 1) * HEAD_DIM)


def head_rows(ref, h, lo, hi, at=slice(None)):
    part = ref[at, lo:hi]
    mask = head_mask(h, 1, lo, hi).astype(F32).astype(BF16)
    return part * jnp.broadcast_to(mask, part.shape)


def dot_nt(a, b):
    return lax.dot_general(a, b, (((1,), (1,)), ((), ())), preferred_element_type=F32)


def dot_nn(a, b):
    return jnp.dot(a, b, preferred_element_type=F32)


def fill_bias(linked_ref, bias_ref):
    here = lax.axis_index("view")
    base, sign = 2 * here, 1 - 2 * (here % 2)
    views = linked_ref.shape[1]
    lane = lax.broadcasted_iota(jnp.int32, (1, bias_ref.shape[1] // BLOCKS), 1)
    half = bias_ref.shape[1] // BLOCKS // 2
    for local in range(2):
        for b, offset in enumerate((0, 2, 4, -2, -4)):
            shifts = []
            for other in range(2):
                gap = sign * offset + other - local
                lower = base + local + jnp.minimum(gap, 0)
                size = jnp.abs(gap)
                row = jnp.clip(lower, 0, views - 1)
                column = jnp.clip(size - 1, 0, REACH - 1)
                linked = (linked_ref[column, row] > 0) & (lower >= 0) & (size <= REACH)
                shifts.append(jnp.where(linked | (size == 0), 0.0, FAR).astype(F32))
            at = slice(2 * b * half, 2 * (b + 1) * half)
            bias_ref[local : local + 1, at] = jnp.where(lane < half, shifts[0], shifts[1])


def put_lane(tile, lane, column):
    at = lax.broadcasted_iota(jnp.int32, tile.shape, 1)
    return jnp.where(at == lane, column, tile)


def add_head(total, i, lo, hi, part):
    part = jnp.where(head_mask(i, part.shape[0], lo, hi), part, 0.0)
    total[:, lo:hi] += part


def forward_kernel(after_a, after_b, q_ref, bias_ref, *refs):
    windows = refs[:BLOCKS]
    attn_ref, p_ref, stat_ref, s_ref, total = refs[BLOCKS:]
    rows, width = q_ref.shape
    half = rows // 2
    total[...] = jnp.zeros_like(total)
    for g in range(width // COLS):
        stat = jnp.zeros((rows, 128), F32)
        for i in range(GROUP):
            h = g * GROUP + i
            lo, hi = head_span(h)
            query = head_rows(q_ref, h, lo, hi)
            top = jnp.full((rows, 1), FAR, F32)
            for b, window in enumerate(windows):
                at = slice(b * rows, (b + 1) * rows)
                scores = dot_nt(query, window[:rows, lo:hi]) * (SCALE * LOG2E)
                scores = jnp.concatenate(
                    [scores[:half] + bias_ref[0:1, at], scores[half:] + bias_ref[1:2, at]], axis=0
                )
                s_ref[h % 2, :, at] = scores
                top = jnp.maximum(top, jnp.max(scores, axis=1, keepdims=True))
            norm = jnp.zeros((rows, 1), F32)
            out = jnp.zeros((rows, hi - lo), F32)
            for b, window in enumerate(windows):
                at = slice(b * rows, (b + 1) * rows)
                weights = jnp.exp2(s_ref[h % 2, :, at] - top)
                norm += jnp.sum(weights, axis=1, keepdims=True)
                low = weights.astype(BF16)
                p_ref[h, :, at] = low
                out += dot_nn(low, window[rows:, lo:hi])
            add_head(total, h, lo, hi, out / norm)
            stat = put_lane(stat, i, top + jnp.log2(norm))
            stat = put_lane(stat, GROUP + i, SCALE / norm)
        stat_ref[g] = stat
    attn_ref[...] = total[...].astype(BF16)


def forward(after, q, bias, windows):
    rows, width = q.shape
    groups = width // COLS
    whole = pl.BlockSpec((rows, width), lambda: (0, 0))
    return pl.pallas_call(
        forward_kernel,
        in_specs=[ORDER, ORDER, whole] + [HELD] * (1 + len(windows)),
        out_specs=[HELD] * 3,
        out_shape=[
            jax.ShapeDtypeStruct((rows, width), BF16),
            jax.ShapeDtypeStruct((groups * GROUP, rows, BLOCKS * rows), BF16),
            jax.ShapeDtypeStruct((groups, rows, 128), F32),
        ],
        scratch_shapes=[
            pltpu.VMEM((2, rows, BLOCKS * rows), F32),
            pltpu.VMEM((rows, width), F32),
        ],
        compiler_params=pltpu.CompilerParams(vmem_limit_bytes=VMEM_LIMIT),
        cost_estimate=COST,
        name="forward",
    )(*after, in_hbm(q), *in_vmem((bias, *windows)))


def stage_kernel(linked_ref, w_ref, out_ref, bias_ref, sem):
    copy = pltpu.make_async_copy(w_ref, out_ref, sem)
    copy.start()
    fill_bias(linked_ref, bias_ref)
    copy.wait()


def stage(linked, w_out, rows):
    return pl.pallas_call(
        stage_kernel,
        in_specs=[SCALARS, ORDER],
        out_specs=[HELD] * 2,
        out_shape=[
            jax.ShapeDtypeStruct(w_out.shape, w_out.dtype),
            jax.ShapeDtypeStruct((2, BLOCKS * rows), F32),
        ],
        scratch_shapes=[pltpu.SemaphoreType.DMA],
        compiler_params=pltpu.CompilerParams(vmem_limit_bytes=SMALL_LIMIT),
        cost_estimate=COST,
        name="stage",
    )(linked, in_hbm(w_out))


def columns(w_ref, by):
    width = w_ref.shape[0]
    at = (lax.axis_index("head") + by) % (w_ref.shape[1] // width) * width
    return w_ref[:, pl.ds(pl.multiple_of(at, width), width)]


def d_attn_kernel(d0, d1, d2, d3, w_ref, out_ref):
    total = 0.0
    for by, d_ref in zip((0, 1, 3, 2), (d0, d1, d2, d3)):
        total += dot_nt(d_ref[...], columns(w_ref, by))
    out_ref[...] = total.astype(BF16)


def attn_cotangent(parts, w_held):
    rows, width = parts[0].shape
    whole = pl.BlockSpec((rows, width), lambda: (0, 0))
    return pl.pallas_call(
        d_attn_kernel,
        in_specs=[whole] + [HELD] * 4,
        out_specs=HELD,
        out_shape=jax.ShapeDtypeStruct((rows, width), BF16),
        compiler_params=pltpu.CompilerParams(vmem_limit_bytes=VMEM_LIMIT),
        cost_estimate=declared(C0),
        name="attn_cotangent",
    )(in_hbm(parts[0]), *in_vmem((*parts[1:], w_held)))


def project_kernel(q_ref, attn_ref, d_ref, stat_ref, w_ref, *refs):
    parts, stat_out, message = refs[:4], *refs[4:]
    rows = attn_ref.shape[0]
    message[:rows] = q_ref[...]
    message[rows : 2 * rows] = d_ref[...]
    product = attn_ref[...].astype(F32) * d_ref[...].astype(F32)
    slabs = []
    for g in range(stat_ref.shape[0]):
        stat = stat_ref[g]
        travels = stat
        for i in range(GROUP):
            lo, hi = head_span(i)
            mine = jnp.where(
                head_mask(i, rows, lo, hi), product[:, g * COLS + lo : g * COLS + hi], 0.0
            )
            delta = jnp.sum(mine, axis=1, keepdims=True)
            stat = put_lane(stat, 2 * GROUP + i, delta)
            travels = put_lane(travels, GROUP + i, delta)
        stat_out[g] = stat
        slabs.append(travels.T[: 2 * GROUP])
    rest = jnp.concatenate(slabs, axis=0)
    for n in range(3):
        piece = rest.astype(BF16)
        message[2 * rows :, n * rows : (n + 1) * rows] = piece
        rest = rest - piece.astype(F32)
    for by, out_ref in zip((1, 3, 2, 0), parts):
        out_ref[...] = dot_nn(attn_ref[...], columns(w_ref, by)).astype(out_ref.dtype)


def project(q, attn, d_attn, stat, w_out):
    rows, width = attn.shape
    groups = stat.shape[0]
    return pl.pallas_call(
        project_kernel,
        in_specs=[pl.BlockSpec((rows, width), lambda: (0, 0))] + [HELD] * 4,
        out_specs=[HELD] * 6,
        out_shape=[jax.ShapeDtypeStruct((rows, width), BF16)] * 3
        + [
            jax.ShapeDtypeStruct((rows, width), F32),
            jax.ShapeDtypeStruct((groups, rows, 128), F32),
            jax.ShapeDtypeStruct((2 * rows + STAT_ROWS, width), BF16),
        ],
        compiler_params=pltpu.CompilerParams(vmem_limit_bytes=VMEM_LIMIT),
        cost_estimate=COST,
        name="project",
    )(in_hbm(q), *in_vmem((attn, d_attn, stat, w_out)))


def query_grad_kernel(p_ref, d_ref, stat_ref, *refs):
    windows = refs[:BLOCKS]
    out_ref, total = refs[BLOCKS:]
    rows, width = d_ref.shape
    total[...] = jnp.zeros_like(total)
    for h in range(width // HEAD_DIM):
        g, i = h // GROUP, h % GROUP
        lo, hi = head_span(h)
        cot = head_rows(d_ref, h, lo, hi)
        delta = stat_ref[g, :, 2 * GROUP + i : 2 * GROUP + i + 1]
        scale = stat_ref[g, :, GROUP + i : GROUP + i + 1]
        key = jnp.concatenate([w[:rows, lo:hi] for w in windows])
        value = jnp.concatenate([w[rows:, lo:hi] for w in windows])
        d_probs = dot_nt(cot, value)
        d_scores = (p_ref[h].astype(F32) * (d_probs - delta)).astype(BF16)
        add_head(total, h, lo, hi, dot_nn(d_scores, key) * scale)
    out_ref[...] = total[...].astype(BF16)


def query_grad(p, d_attn, stat, windows):
    rows, width = d_attn.shape
    return pl.pallas_call(
        query_grad_kernel,
        in_specs=[HELD] * (3 + len(windows)),
        out_specs=pl.BlockSpec((rows, width), lambda: (0, 0)),
        out_shape=jax.ShapeDtypeStruct((rows, width), BF16),
        scratch_shapes=[pltpu.VMEM((rows, width), F32)],
        compiler_params=pltpu.CompilerParams(vmem_limit_bytes=VMEM_LIMIT),
        cost_estimate=declared(C3),
        name="query_grad",
    )(*in_vmem((p, d_attn, stat, *windows)))


def key_grad_kernel(blocks, bias_ref, kv_ref, *refs):
    count = len(blocks)
    messages = refs[:count]
    *so_far, gk_ref, gv_ref, total_k, total_v = refs[count:]
    final = len(so_far) > 2
    if final:
        so_far, out_ref = so_far[:-1], so_far[-1]
        add_parts(*so_far[2:], out_ref)
    rows, width = kv_ref.shape[0] // 2, kv_ref.shape[1]
    half = rows // 2
    stats = []
    for message in messages:
        packed = message[2 * rows :].astype(F32)
        stats.append(packed[:, :rows] + packed[:, rows : 2 * rows] + packed[:, 2 * rows :])
    stats = jnp.concatenate(stats, axis=1)
    bias = jnp.concatenate([bias_ref[:, b * rows : (b + 1) * rows] for b in blocks], axis=1)
    for total, ref in zip((total_k, total_v), so_far[:2] if len(so_far) > 1 else (None, None)):
        total[...] = jnp.zeros_like(total) if ref is None else ref[...]
    for h in range(width // HEAD_DIM):
        lo, hi = head_span(h)
        at_lse = h // GROUP * 2 * GROUP + h % GROUP
        at_delta = at_lse + GROUP
        key = head_rows(kv_ref, h, lo, hi, slice(0, rows))
        value = head_rows(kv_ref, h, lo, hi, slice(rows, 2 * rows))
        query = jnp.concatenate([ref[:rows, lo:hi] for ref in messages])
        cot = jnp.concatenate([ref[rows : 2 * rows, lo:hi] for ref in messages])
        shift = bias - stats[at_lse : at_lse + 1]
        delta = stats[at_delta : at_delta + 1]
        scores = dot_nt(key, query) * (SCALE * LOG2E)
        weights = jnp.exp2(
            jnp.concatenate([scores[:half] + shift[0:1], scores[half:] + shift[1:2]], axis=0)
        )
        grad_v = dot_nn(weights.astype(BF16), cot)
        d_probs = dot_nt(value, cot)
        grad_k = dot_nn((weights * (d_probs - delta)).astype(BF16), query)
        add_head(total_k, h, lo, hi, grad_k)
        add_head(total_v, h, lo, hi, grad_v)
    gk_ref[...] = (total_k[...] * SCALE if final else total_k[...]).astype(gk_ref.dtype)
    gv_ref[...] = total_v[...].astype(gv_ref.dtype)


def add_parts(own, a, b, c, out_ref):
    total = own[...] + a[...].astype(F32) + b[...].astype(F32) + c[...].astype(F32)
    out_ref[...] = total.astype(BF16)


def key_grad(name, blocks, bias, kv, messages, so_far=(), parts=()):
    rows, width = kv.shape[0] // 2, kv.shape[1]
    whole = pl.BlockSpec((rows, width), lambda: (0, 0))
    held = (bias, kv, *messages, *so_far, *parts)
    gives = [whole] * 3 if parts else [HELD] * 2
    return pl.pallas_call(
        partial(key_grad_kernel, blocks),
        in_specs=[HELD] * len(held),
        out_specs=gives,
        out_shape=[jax.ShapeDtypeStruct((rows, width), BF16 if parts else F32)] * len(gives),
        scratch_shapes=[pltpu.VMEM((rows, width), F32)] * 2,
        compiler_params=pltpu.CompilerParams(vmem_limit_bytes=VMEM_LIMIT),
        cost_estimate=COST,
        name=name,
    )(*in_vmem(held))


def gate_kernel(*refs):
    pass


def gate(arrays, after=(), cost=COST):
    return pl.pallas_call(
        gate_kernel,
        in_specs=[ORDER] * (len(arrays) + len(after)),
        out_specs=[ORDER] * len(arrays),
        out_shape=[jax.ShapeDtypeStruct(a.shape, a.dtype) for a in arrays],
        input_output_aliases={n: n for n in range(len(arrays))},
        compiler_params=pltpu.CompilerParams(vmem_limit_bytes=SMALL_LIMIT),
        cost_estimate=cost,
        name="gate",
    )(*in_vmem(arrays), *after)


def corner_kernel(*refs):
    refs[-1][...] = jnp.zeros_like(refs[-1])


def corner(array, devices):
    shape = (16, 128)
    tile = pl.pallas_call(
        corner_kernel,
        in_specs=[ORDER],
        out_specs=pl.BlockSpec(shape, lambda: (0, 0)),
        out_shape=jax.ShapeDtypeStruct(shape, BF16),
        compiler_params=pltpu.CompilerParams(vmem_limit_bytes=SMALL_LIMIT),
        cost_estimate=COST,
        name="corner",
    )(array)
    return to_sibling(tile, devices)


def pack_kernel(k_ref, v_ref, out_ref, sems):
    rows = k_ref.shape[0]
    copies = [
        pltpu.make_async_copy(ref, out_ref.at[n * rows : (n + 1) * rows], sems.at[n])
        for n, ref in enumerate((k_ref, v_ref))
    ]
    for copy in copies:
        copy.start()
    for copy in copies:
        copy.wait()


def pack(k, v):
    rows, width = k.shape
    return pl.pallas_call(
        pack_kernel,
        in_specs=[ORDER] * 2,
        out_specs=HELD,
        out_shape=jax.ShapeDtypeStruct((2 * rows, width), BF16),
        scratch_shapes=[pltpu.SemaphoreType.DMA((2,))],
        compiler_params=pltpu.CompilerParams(vmem_limit_bytes=SMALL_LIMIT),
        cost_estimate=COST,
        name="pack",
    )(in_hbm(k), in_hbm(v))


def body(queries, keys, values, d_out, w_out, intersection):
    count, length, width = queries.shape
    devices = lax.axis_size("view")
    groups = lax.axis_size("head")
    q, k, v, d = (a.reshape(count * length, width) for a in (queries, keys, values, d_out))

    def from_group(array, by):
        return send(array, "head", [(i, (i - by) % groups) for i in range(groups)])

    gathered = [from_group(d, by) for by in (1, 3, 2)]
    kv = pack(k, v)
    kv_a, kv_b = from_chip_a(kv, devices), from_chip_b(kv, devices)
    w_held, bias = stage(intersection.T, w_out, count * length)
    (kv_a,) = gate((kv_a,), (w_held,))
    windows = (kv, to_sibling(kv, devices), kv_a, to_sibling(kv_a, devices), kv_b)
    d_attn = attn_cotangent([d] + gathered, w_held)
    attn, p, stat = forward((d_attn, corner(kv_b, devices)), q, bias, windows)
    to_next, to_last, to_far, own, stat, message = project(q, attn, d_attn, stat, w_held)
    d_a, d_b = from_chip_a(message, devices), from_chip_b(message, devices)
    gained = [from_group(part, by) for part, by in ((to_next, 3), (to_last, 1), (to_far, 2))]
    grad_q = query_grad(p, d_attn, stat, windows)
    near = (message, to_sibling(message, devices))
    part = key_grad("key_grad_near", (0, 1), bias, kv, near)
    d_a, d_b = gate((d_a, d_b), (in_hbm(grad_q), part[0]))
    part = key_grad("key_grad_far", (2, 4), bias, kv, (d_a, d_b), part)
    d_last = to_sibling(d_a, devices)
    gained = gate(gained, part[:1], declared(C2))
    attended, grad_k, grad_v = key_grad(
        "key_grad_last", (3,), bias, kv, (d_last,), part, (own, *gained)
    )
    shape = (count, length, width)
    return tuple(a.reshape(shape) for a in (attended, grad_q, grad_k, grad_v))


def solution(mesh):
    columns = P("view", None, "head")
    return jax.shard_map(
        body,
        mesh=mesh,
        in_specs=(columns, columns, columns, columns, P("head", None), P()),
        out_specs=(columns, columns, columns, columns),
        check_vma=False,
    )
```

```python
from functools import partial

import jax
import jax.numpy as jnp
from jax import lax
from jax.experimental import pallas as pl
from jax.experimental.pallas import tpu as pltpu
from jax.sharding import PartitionSpec as P

HEAD_DIM = 96
REACH = 4
GROUP = 4
COLS = GROUP * HEAD_DIM
BLOCKS = 5
SCALE = HEAD_DIM ** (-0.5)
LOG2E = 1.4426950408889634
FAR = -1e30
VMEM_LIMIT = 18 * 1024 * 1024
SMALL_LIMIT = 1024 * 1024
BF16 = jnp.bfloat16
F32 = jnp.float32
SCALARS = pl.BlockSpec(memory_space=pltpu.SMEM)
COST = pl.CostEstimate(flops=1000, bytes_accessed=1000, transcendentals=0)


def declared(units):
    return pl.CostEstimate(flops=units * 300_000_000, bytes_accessed=1000, transcendentals=0)


ORDER = pl.BlockSpec(memory_space=pl.ANY)
HELD = pl.BlockSpec(memory_space=pltpu.VMEM)
STAT_ROWS = 16


def send(array, axis, pairs):
    return lax.ppermute(array, axis, pairs)


def to_sibling(array, count):
    return send(array, "view", [(i, i ^ 1) for i in range(count)])


def from_chip_a(array, count):
    return send(array, "view", [(i, (i + (2 if i % 2 else -2)) % count) for i in range(count)])


def from_chip_b(array, count):
    return send(array, "view", [(i, (i + (-2 if i % 2 else 2)) % count) for i in range(count)])


def in_hbm(array):
    return pltpu.with_memory_space_constraint(array, pltpu.HBM)


def in_vmem(arrays):
    return [pltpu.with_memory_space_constraint(a, pltpu.VMEM) for a in arrays]


def head_span(h):
    lo = h * HEAD_DIM // 128 * 128
    hi = -(-(h + 1) * HEAD_DIM // 128) * 128
    return lo, hi


def head_mask(i, rows, lo, hi):
    lane = lax.broadcasted_iota(jnp.int32, (rows, hi - lo), 1) + lo
    return (lane >= i * HEAD_DIM) & (lane < (i + 1) * HEAD_DIM)


def head_rows(ref, h, lo, hi, at=slice(None)):
    part = ref[at, lo:hi]
    mask = head_mask(h, 1, lo, hi).astype(F32).astype(BF16)
    return part * jnp.broadcast_to(mask, part.shape)


def dot_nt(a, b):
    return lax.dot_general(a, b, (((1,), (1,)), ((), ())), preferred_element_type=F32)


def dot_nn(a, b):
    return jnp.dot(a, b, preferred_element_type=F32)


def fill_bias(linked_ref, bias_ref):
    here = lax.axis_index("view")
    base, sign = 2 * here, 1 - 2 * (here % 2)
    views = linked_ref.shape[1]
    lane = lax.broadcasted_iota(jnp.int32, (1, bias_ref.shape[1] // BLOCKS), 1)
    half = bias_ref.shape[1] // BLOCKS // 2
    for local in range(2):
        for b, offset in enumerate((0, 2, 4, -2, -4)):
            shifts = []
            for other in range(2):
                gap = sign * offset + other - local
                lower = base + local + jnp.minimum(gap, 0)
                size = jnp.abs(gap)
                row = jnp.clip(lower, 0, views - 1)
                column = jnp.clip(size - 1, 0, REACH - 1)
                linked = (linked_ref[column, row] > 0) & (lower >= 0) & (size <= REACH)
                shifts.append(jnp.where(linked | (size == 0), 0.0, FAR).astype(F32))
            at = slice(2 * b * half, 2 * (b + 1) * half)
            bias_ref[local : local + 1, at] = jnp.where(lane < half, shifts[0], shifts[1])


def put_lane(tile, lane, column):
    at = lax.broadcasted_iota(jnp.int32, tile.shape, 1)
    return jnp.where(at == lane, column, tile)


def add_head(total, i, lo, hi, part):
    part = jnp.where(head_mask(i, part.shape[0], lo, hi), part, 0.0)
    total[:, lo:hi] += part


CHUNKS = ((0, 2), (2, 4), (4, 5))


def forward_kernel(after_a, after_b, q_ref, bias_ref, *refs):
    windows = refs[:BLOCKS]
    attn_ref, p_ref, stat_ref, s_ref, total = refs[BLOCKS:]
    rows, width = q_ref.shape
    half = rows // 2
    total[...] = jnp.zeros_like(total)
    for g in range(width // COLS):
        stat = jnp.zeros((rows, 128), F32)
        for i in range(GROUP):
            h = g * GROUP + i
            lo, hi = head_span(h)
            query = head_rows(q_ref, h, lo, hi)
            top = jnp.full((rows, 1), FAR, F32)
            for first, past in CHUNKS:
                at = slice(first * rows, past * rows)
                key = jnp.concatenate([w[:rows, lo:hi] for w in windows[first:past]])
                scores = dot_nt(query, key) * (SCALE * LOG2E)
                scores = jnp.concatenate(
                    [scores[:half] + bias_ref[0:1, at], scores[half:] + bias_ref[1:2, at]], axis=0
                )
                s_ref[h % 2, :, at] = scores
                top = jnp.maximum(top, jnp.max(scores, axis=1, keepdims=True))
            norm = jnp.zeros((rows, 1), F32)
            out = jnp.zeros((rows, hi - lo), F32)
            for first, past in CHUNKS:
                at = slice(first * rows, past * rows)
                weights = jnp.exp2(s_ref[h % 2, :, at] - top)
                norm += jnp.sum(weights, axis=1, keepdims=True)
                low = weights.astype(BF16)
                p_ref[h, :, at] = low
                out += dot_nn(low, jnp.concatenate([w[rows:, lo:hi] for w in windows[first:past]]))
            add_head(total, h, lo, hi, out / norm)
            stat = put_lane(stat, i, top + jnp.log2(norm))
            stat = put_lane(stat, GROUP + i, SCALE / norm)
        stat_ref[g] = stat
    attn_ref[...] = total[...].astype(BF16)


def forward(after, q, bias, windows):
    rows, width = q.shape
    groups = width // COLS
    whole = pl.BlockSpec((rows, width), lambda: (0, 0))
    return pl.pallas_call(
        forward_kernel,
        in_specs=[ORDER, ORDER] + [HELD] * (2 + len(windows)),
        out_specs=[HELD] * 3,
        out_shape=[
            jax.ShapeDtypeStruct((rows, width), BF16),
            jax.ShapeDtypeStruct((groups * GROUP, rows, BLOCKS * rows), BF16),
            jax.ShapeDtypeStruct((groups, rows, 128), F32),
        ],
        scratch_shapes=[
            pltpu.VMEM((2, rows, BLOCKS * rows), F32),
            pltpu.VMEM((rows, width), F32),
        ],
        compiler_params=pltpu.CompilerParams(vmem_limit_bytes=VMEM_LIMIT),
        cost_estimate=COST,
        name="forward",
    )(*after, *in_vmem((q, bias, *windows)))


def stage_kernel(linked_ref, w_ref, d_ref, q_ref, w_out, d_out, q_out, bias_ref, sems):
    pairs = ((w_ref, w_out), (d_ref, d_out), (q_ref, q_out))
    copies = [pltpu.make_async_copy(*pair, sems.at[n]) for n, pair in enumerate(pairs)]
    for copy in copies:
        copy.start()
    fill_bias(linked_ref, bias_ref)
    for copy in copies:
        copy.wait()


def stage(linked, w_out, d, q):
    arrays = (w_out, d, q)
    return pl.pallas_call(
        stage_kernel,
        in_specs=[SCALARS] + [ORDER] * 3,
        out_specs=[HELD] * 4,
        out_shape=[jax.ShapeDtypeStruct(a.shape, a.dtype) for a in arrays]
        + [jax.ShapeDtypeStruct((2, BLOCKS * q.shape[0]), F32)],
        scratch_shapes=[pltpu.SemaphoreType.DMA((3,))],
        compiler_params=pltpu.CompilerParams(vmem_limit_bytes=SMALL_LIMIT),
        cost_estimate=COST,
        name="stage",
    )(linked, *(in_hbm(a) for a in arrays))


def columns(w_ref, by):
    width = w_ref.shape[0]
    at = (lax.axis_index("head") + by) % (w_ref.shape[1] // width) * width
    return w_ref[:, pl.ds(pl.multiple_of(at, width), width)]


def d_attn_kernel(d0, d1, d2, d3, w_ref, out_ref):
    total = 0.0
    for by, d_ref in zip((0, 1, 3, 2), (d0, d1, d2, d3)):
        total += dot_nt(d_ref[...], columns(w_ref, by))
    out_ref[...] = total.astype(BF16)


def attn_cotangent(parts, w_held):
    rows, width = parts[0].shape
    return pl.pallas_call(
        d_attn_kernel,
        in_specs=[HELD] * 5,
        out_specs=HELD,
        out_shape=jax.ShapeDtypeStruct((rows, width), BF16),
        compiler_params=pltpu.CompilerParams(vmem_limit_bytes=VMEM_LIMIT),
        cost_estimate=declared(20),
        name="attn_cotangent",
    )(*in_vmem((*parts, w_held)))


def message_kernel(q_ref, attn_ref, d_ref, stat_ref, stat_out, message, sems):
    rows = attn_ref.shape[0]
    copies = [
        pltpu.make_async_copy(ref, message.at[n * rows : (n + 1) * rows], sems.at[n])
        for n, ref in enumerate((q_ref, d_ref))
    ]
    for copy in copies:
        copy.start()
    product = attn_ref[...].astype(F32) * d_ref[...].astype(F32)
    slabs = []
    for g in range(stat_ref.shape[0]):
        stat = stat_ref[g]
        travels = stat
        for i in range(GROUP):
            lo, hi = head_span(i)
            mine = jnp.where(
                head_mask(i, rows, lo, hi), product[:, g * COLS + lo : g * COLS + hi], 0.0
            )
            delta = jnp.sum(mine, axis=1, keepdims=True)
            stat = put_lane(stat, 2 * GROUP + i, delta)
            travels = put_lane(travels, GROUP + i, delta)
        stat_out[g] = stat
        slabs.append(travels.T[: 2 * GROUP])
    rest = jnp.concatenate(slabs, axis=0)
    for n in range(3):
        piece = rest.astype(BF16)
        message[2 * rows :, n * rows : (n + 1) * rows] = piece
        rest = rest - piece.astype(F32)
    for copy in copies:
        copy.wait()


def make_message(q, attn, d_attn, stat):
    rows, width = attn.shape
    return pl.pallas_call(
        message_kernel,
        in_specs=[HELD] * 4,
        out_specs=[HELD] * 2,
        out_shape=[
            jax.ShapeDtypeStruct(stat.shape, F32),
            jax.ShapeDtypeStruct((2 * rows + STAT_ROWS, width), BF16),
        ],
        scratch_shapes=[pltpu.SemaphoreType.DMA((2,))],
        compiler_params=pltpu.CompilerParams(vmem_limit_bytes=VMEM_LIMIT),
        cost_estimate=COST,
        name="message",
    )(*in_vmem((q, attn, d_attn, stat)))


def project_kernel(attn_ref, w_ref, *parts):
    for by, out_ref in zip((1, 3, 2, 0), parts):
        out_ref[...] = dot_nn(attn_ref[...], columns(w_ref, by)).astype(out_ref.dtype)


def project(attn, w_out):
    return pl.pallas_call(
        project_kernel,
        in_specs=[HELD] * 2,
        out_specs=[HELD] * 4,
        out_shape=[jax.ShapeDtypeStruct(attn.shape, BF16)] * 3
        + [jax.ShapeDtypeStruct(attn.shape, F32)],
        compiler_params=pltpu.CompilerParams(vmem_limit_bytes=VMEM_LIMIT),
        cost_estimate=COST,
        name="project",
    )(*in_vmem((attn, w_out)))


def query_grad_kernel(p_ref, d_ref, stat_ref, *refs):
    windows = refs[:BLOCKS]
    out_ref, total = refs[BLOCKS:]
    rows, width = d_ref.shape
    total[...] = jnp.zeros_like(total)
    for h in range(width // HEAD_DIM):
        g, i = h // GROUP, h % GROUP
        lo, hi = head_span(h)
        cot = head_rows(d_ref, h, lo, hi)
        delta = stat_ref[g, :, 2 * GROUP + i : 2 * GROUP + i + 1]
        scale = stat_ref[g, :, GROUP + i : GROUP + i + 1]
        key = jnp.concatenate([w[:rows, lo:hi] for w in windows])
        value = jnp.concatenate([w[rows:, lo:hi] for w in windows])
        d_probs = dot_nt(cot, value)
        d_scores = (p_ref[h].astype(F32) * (d_probs - delta)).astype(BF16)
        add_head(total, h, lo, hi, dot_nn(d_scores, key) * scale)
    out_ref[...] = total[...].astype(BF16)


def query_grad(p, d_attn, stat, windows):
    rows, width = d_attn.shape
    return pl.pallas_call(
        query_grad_kernel,
        in_specs=[HELD] * (3 + len(windows)),
        out_specs=pl.BlockSpec((rows, width), lambda: (0, 0)),
        out_shape=jax.ShapeDtypeStruct((rows, width), BF16),
        scratch_shapes=[pltpu.VMEM((rows, width), F32)],
        compiler_params=pltpu.CompilerParams(vmem_limit_bytes=VMEM_LIMIT),
        cost_estimate=declared(1),
        name="query_grad",
    )(*in_vmem((p, d_attn, stat, *windows)))


def key_grad_kernel(blocks, bias_ref, kv_ref, *refs):
    count = len(blocks)
    messages = refs[:count]
    *so_far, gk_ref, gv_ref, total_k, total_v = refs[count:]
    final = len(so_far) > 2
    if final:
        so_far, out_ref = so_far[:-1], so_far[-1]
        add_parts(*so_far[2:], out_ref)
    rows, width = kv_ref.shape[0] // 2, kv_ref.shape[1]
    half = rows // 2
    stats = []
    for message in messages:
        packed = message[2 * rows :].astype(F32)
        stats.append(packed[:, :rows] + packed[:, rows : 2 * rows] + packed[:, 2 * rows :])
    stats = jnp.concatenate(stats, axis=1)
    bias = jnp.concatenate([bias_ref[:, b * rows : (b + 1) * rows] for b in blocks], axis=1)
    for total, ref in zip((total_k, total_v), so_far[:2] if len(so_far) > 1 else (None, None)):
        total[...] = jnp.zeros_like(total) if ref is None else ref[...]
    for h in range(width // HEAD_DIM):
        lo, hi = head_span(h)
        at_lse = h // GROUP * 2 * GROUP + h % GROUP
        at_delta = at_lse + GROUP
        key = head_rows(kv_ref, h, lo, hi, slice(0, rows))
        value = head_rows(kv_ref, h, lo, hi, slice(rows, 2 * rows))
        query = jnp.concatenate([ref[:rows, lo:hi] for ref in messages])
        cot = jnp.concatenate([ref[rows : 2 * rows, lo:hi] for ref in messages])
        shift = bias - stats[at_lse : at_lse + 1]
        delta = stats[at_delta : at_delta + 1]
        scores = dot_nt(key, query) * (SCALE * LOG2E)
        weights = jnp.exp2(
            jnp.concatenate([scores[:half] + shift[0:1], scores[half:] + shift[1:2]], axis=0)
        )
        grad_v = dot_nn(weights.astype(BF16), cot)
        d_probs = dot_nt(value, cot)
        grad_k = dot_nn((weights * (d_probs - delta)).astype(BF16), query)
        add_head(total_k, h, lo, hi, grad_k)
        add_head(total_v, h, lo, hi, grad_v)
    gk_ref[...] = (total_k[...] * SCALE if final else total_k[...]).astype(gk_ref.dtype)
    gv_ref[...] = total_v[...].astype(gv_ref.dtype)


def add_parts(own, a, b, c, out_ref):
    total = own[...] + a[...].astype(F32) + b[...].astype(F32) + c[...].astype(F32)
    out_ref[...] = total.astype(BF16)


def key_grad(name, blocks, bias, kv, messages, so_far=(), parts=()):
    rows, width = kv.shape[0] // 2, kv.shape[1]
    whole = pl.BlockSpec((rows, width), lambda: (0, 0))
    held = (bias, kv, *messages, *so_far, *parts)
    gives = [whole] * 3 if parts else [HELD] * 2
    return pl.pallas_call(
        partial(key_grad_kernel, blocks),
        in_specs=[HELD] * len(held),
        out_specs=gives,
        out_shape=[jax.ShapeDtypeStruct((rows, width), BF16 if parts else F32)] * len(gives),
        scratch_shapes=[pltpu.VMEM((rows, width), F32)] * 2,
        compiler_params=pltpu.CompilerParams(vmem_limit_bytes=VMEM_LIMIT),
        cost_estimate=COST,
        name=name,
    )(*in_vmem(held))


def gate_kernel(*refs):
    pass


def gate(arrays, after=(), cost=COST):
    return pl.pallas_call(
        gate_kernel,
        in_specs=[ORDER] * (len(arrays) + len(after)),
        out_specs=[ORDER] * len(arrays),
        out_shape=[jax.ShapeDtypeStruct(a.shape, a.dtype) for a in arrays],
        input_output_aliases={n: n for n in range(len(arrays))},
        compiler_params=pltpu.CompilerParams(vmem_limit_bytes=SMALL_LIMIT),
        cost_estimate=cost,
        name="gate",
    )(*in_vmem(arrays), *after)


def corner_kernel(*refs):
    refs[-1][...] = jnp.zeros_like(refs[-1])


def corner(array, devices):
    shape = (16, 128)
    tile = pl.pallas_call(
        corner_kernel,
        in_specs=[ORDER],
        out_specs=pl.BlockSpec(shape, lambda: (0, 0)),
        out_shape=jax.ShapeDtypeStruct(shape, BF16),
        compiler_params=pltpu.CompilerParams(vmem_limit_bytes=SMALL_LIMIT),
        cost_estimate=COST,
        name="corner",
    )(array)
    return to_sibling(tile, devices)


def pack_kernel(k_ref, v_ref, out_ref, sems):
    rows = k_ref.shape[0]
    copies = [
        pltpu.make_async_copy(ref, out_ref.at[n * rows : (n + 1) * rows], sems.at[n])
        for n, ref in enumerate((k_ref, v_ref))
    ]
    for copy in copies:
        copy.start()
    for copy in copies:
        copy.wait()


def pack(k, v):
    rows, width = k.shape
    return pl.pallas_call(
        pack_kernel,
        in_specs=[ORDER] * 2,
        out_specs=HELD,
        out_shape=jax.ShapeDtypeStruct((2 * rows, width), BF16),
        scratch_shapes=[pltpu.SemaphoreType.DMA((2,))],
        compiler_params=pltpu.CompilerParams(vmem_limit_bytes=SMALL_LIMIT),
        cost_estimate=COST,
        name="pack",
    )(in_hbm(k), in_hbm(v))


def body(queries, keys, values, d_out, w_out, intersection):
    count, length, width = queries.shape
    devices = lax.axis_size("view")
    groups = lax.axis_size("head")
    q, k, v, d = (a.reshape(count * length, width) for a in (queries, keys, values, d_out))

    def from_group(array, by):
        return send(array, "head", [(i, (i - by) % groups) for i in range(groups)])

    gathered = [from_group(d, by) for by in (1, 3, 2)]
    kv = pack(k, v)
    kv_a, kv_b = from_chip_a(kv, devices), from_chip_b(kv, devices)
    w_held, d, q, bias = stage(intersection.T, w_out, d, q)
    (kv_a,) = gate((kv_a,), (w_held,))
    windows = (kv, to_sibling(kv, devices), kv_a, to_sibling(kv_a, devices), kv_b)
    d_attn = attn_cotangent([d] + gathered, w_held)
    attn, p, stat = forward((d_attn, corner(kv_b, devices)), q, bias, windows)
    stat, message = make_message(q, attn, d_attn, stat)
    to_next, to_last, to_far, own = project(attn, w_held)
    d_a, d_b = from_chip_a(message, devices), from_chip_b(message, devices)
    gained = [from_group(part, by) for part, by in ((to_next, 3), (to_last, 1), (to_far, 2))]
    grad_q = query_grad(p, d_attn, stat, windows)
    near = (message, to_sibling(message, devices))
    part = key_grad("key_grad_near", (0, 1), bias, kv, near)
    d_a, d_b = gate((d_a, d_b), (in_hbm(grad_q), part[0]))
    part = key_grad("key_grad_far", (2, 4), bias, kv, (d_a, d_b), part)
    d_last = to_sibling(d_a, devices)
    gained = gate(gained, part[:1], declared(30))
    attended, grad_k, grad_v = key_grad(
        "key_grad_last", (3,), bias, kv, (d_last,), part, (own, *gained)
    )
    shape = (count, length, width)
    return tuple(a.reshape(shape) for a in (attended, grad_q, grad_k, grad_v))


def solution(mesh):
    columns = P("view", None, "head")
    return jax.shard_map(
        body,
        mesh=mesh,
        in_specs=(columns, columns, columns, columns, P("head", None), P()),
        out_specs=(columns, columns, columns, columns),
        check_vma=False,
    )
```

```python
from functools import partial

import jax
import jax.numpy as jnp
from jax import lax
from jax.experimental import pallas as pl
from jax.experimental.pallas import tpu as pltpu
from jax.sharding import PartitionSpec as P

HEAD_DIM = 96
REACH = 4
GROUP = 4
COLS = GROUP * HEAD_DIM
BLOCKS = 5
SCALE = HEAD_DIM ** (-0.5)
LOG2E = 1.4426950408889634
FAR = -1e30
VMEM_LIMIT = 18 * 1024 * 1024
SMALL_LIMIT = 1024 * 1024
BF16 = jnp.bfloat16
F32 = jnp.float32
SCALARS = pl.BlockSpec(memory_space=pltpu.SMEM)
COST = pl.CostEstimate(flops=1000, bytes_accessed=1000, transcendentals=0)


def declared(units):
    return pl.CostEstimate(flops=units * 300_000_000, bytes_accessed=1000, transcendentals=0)


ORDER = pl.BlockSpec(memory_space=pl.ANY)
HELD = pl.BlockSpec(memory_space=pltpu.VMEM)
STAT_ROWS = 16


def send(array, axis, pairs):
    return lax.ppermute(array, axis, pairs)


def to_sibling(array, count):
    return send(array, "view", [(i, i ^ 1) for i in range(count)])


def from_chip_a(array, count):
    return send(array, "view", [(i, (i + (2 if i % 2 else -2)) % count) for i in range(count)])


def from_chip_b(array, count):
    return send(array, "view", [(i, (i + (-2 if i % 2 else 2)) % count) for i in range(count)])


def in_hbm(array):
    return pltpu.with_memory_space_constraint(array, pltpu.HBM)


def in_vmem(arrays):
    return [pltpu.with_memory_space_constraint(a, pltpu.VMEM) for a in arrays]


def head_span(h):
    lo = h * HEAD_DIM // 128 * 128
    hi = -(-(h + 1) * HEAD_DIM // 128) * 128
    return lo, hi


def head_mask(i, rows, lo, hi):
    lane = lax.broadcasted_iota(jnp.int32, (rows, hi - lo), 1) + lo
    return (lane >= i * HEAD_DIM) & (lane < (i + 1) * HEAD_DIM)


def head_rows(ref, h, lo, hi, at=slice(None)):
    part = ref[at, lo:hi]
    mask = head_mask(h, 1, lo, hi).astype(F32).astype(BF16)
    return part * jnp.broadcast_to(mask, part.shape)


def dot_nt(a, b):
    return lax.dot_general(a, b, (((1,), (1,)), ((), ())), preferred_element_type=F32)


def dot_nn(a, b):
    return jnp.dot(a, b, preferred_element_type=F32)


def fill_bias(linked_ref, bias_ref):
    here = lax.axis_index("view")
    base, sign = 2 * here, 1 - 2 * (here % 2)
    views = linked_ref.shape[1]
    lane = lax.broadcasted_iota(jnp.int32, (1, bias_ref.shape[1] // BLOCKS), 1)
    half = bias_ref.shape[1] // BLOCKS // 2
    for local in range(2):
        for b, offset in enumerate((0, 2, 4, -2, -4)):
            shifts = []
            for other in range(2):
                gap = sign * offset + other - local
                lower = base + local + jnp.minimum(gap, 0)
                size = jnp.abs(gap)
                row = jnp.clip(lower, 0, views - 1)
                column = jnp.clip(size - 1, 0, REACH - 1)
                linked = (linked_ref[column, row] > 0) & (lower >= 0) & (size <= REACH)
                shifts.append(jnp.where(linked | (size == 0), 0.0, FAR).astype(F32))
            at = slice(2 * b * half, 2 * (b + 1) * half)
            bias_ref[local : local + 1, at] = jnp.where(lane < half, shifts[0], shifts[1])


def put_lane(tile, lane, column):
    at = lax.broadcasted_iota(jnp.int32, tile.shape, 1)
    return jnp.where(at == lane, column, tile)


def add_head(total, i, lo, hi, part):
    part = jnp.where(head_mask(i, part.shape[0], lo, hi), part, 0.0)
    total[:, lo:hi] += part


CHUNKS = ((0, 3), (3, 5))


def forward_kernel(after_ref, q_ref, bias_ref, *refs):
    windows = refs[:BLOCKS]
    attn_ref, p_ref, stat_ref, s_ref, total = refs[BLOCKS:]
    rows, width = q_ref.shape
    half = rows // 2
    total[...] = jnp.zeros_like(total)
    for g in range(width // COLS):
        stat = jnp.zeros((rows, 128), F32)
        for i in range(GROUP):
            h = g * GROUP + i
            lo, hi = head_span(h)
            query = head_rows(q_ref, h, lo, hi)
            top = jnp.full((rows, 1), FAR, F32)
            for first, past in CHUNKS:
                at = slice(first * rows, past * rows)
                key = jnp.concatenate([w[:rows, lo:hi] for w in windows[first:past]])
                scores = dot_nt(query, key) * (SCALE * LOG2E)
                scores = jnp.concatenate(
                    [scores[:half] + bias_ref[0:1, at], scores[half:] + bias_ref[1:2, at]], axis=0
                )
                s_ref[h % 2, :, at] = scores
                top = jnp.maximum(top, jnp.max(scores, axis=1, keepdims=True))
            norm = jnp.zeros((rows, 1), F32)
            out = jnp.zeros((rows, hi - lo), F32)
            for first, past in CHUNKS:
                at = slice(first * rows, past * rows)
                weights = jnp.exp2(s_ref[h % 2, :, at] - top)
                norm += jnp.sum(weights, axis=1, keepdims=True)
                low = weights.astype(BF16)
                p_ref[h, :, at] = low
                out += dot_nn(low, jnp.concatenate([w[rows:, lo:hi] for w in windows[first:past]]))
            add_head(total, h, lo, hi, out / norm)
            stat = put_lane(stat, i, top + jnp.log2(norm))
            stat = put_lane(stat, GROUP + i, SCALE / norm)
        stat_ref[g] = stat
    attn_ref[...] = total[...].astype(BF16)


def forward(after, q, bias, windows):
    rows, width = q.shape
    groups = width // COLS
    whole = pl.BlockSpec((rows, width), lambda: (0, 0))
    return pl.pallas_call(
        forward_kernel,
        in_specs=[ORDER] + [HELD] * (2 + len(windows)),
        out_specs=[HELD] * 3,
        out_shape=[
            jax.ShapeDtypeStruct((rows, width), BF16),
            jax.ShapeDtypeStruct((groups * GROUP, rows, BLOCKS * rows), BF16),
            jax.ShapeDtypeStruct((groups, rows, 128), F32),
        ],
        scratch_shapes=[
            pltpu.VMEM((2, rows, BLOCKS * rows), F32),
            pltpu.VMEM((rows, width), F32),
        ],
        compiler_params=pltpu.CompilerParams(vmem_limit_bytes=VMEM_LIMIT),
        cost_estimate=COST,
        name="forward",
    )(after, *in_vmem((q, bias, *windows)))


def stage_kernel(linked_ref, w_ref, d_ref, q_ref, w_out, d_out, q_out, bias_ref, sems):
    pairs = ((w_ref, w_out), (d_ref, d_out), (q_ref, q_out))
    copies = [pltpu.make_async_copy(*pair, sems.at[n]) for n, pair in enumerate(pairs)]
    for copy in copies:
        copy.start()
    fill_bias(linked_ref, bias_ref)
    for copy in copies:
        copy.wait()


def stage(linked, w_out, d, q):
    arrays = (w_out, d, q)
    return pl.pallas_call(
        stage_kernel,
        in_specs=[SCALARS] + [ORDER] * 3,
        out_specs=[HELD] * 4,
        out_shape=[jax.ShapeDtypeStruct(a.shape, a.dtype) for a in arrays]
        + [jax.ShapeDtypeStruct((2, BLOCKS * q.shape[0]), F32)],
        scratch_shapes=[pltpu.SemaphoreType.DMA((3,))],
        compiler_params=pltpu.CompilerParams(vmem_limit_bytes=SMALL_LIMIT),
        cost_estimate=COST,
        name="stage",
    )(linked, *(in_hbm(a) for a in arrays))


def columns(w_ref, by):
    width = w_ref.shape[0]
    at = (lax.axis_index("head") + by) % (w_ref.shape[1] // width) * width
    return w_ref[:, pl.ds(pl.multiple_of(at, width), width)]


def d_attn_kernel(d0, d1, d2, d3, w_ref, out_ref):
    total = 0.0
    for by, d_ref in zip((0, 1, 3, 2), (d0, d1, d2, d3)):
        total += dot_nt(d_ref[...], columns(w_ref, by))
    out_ref[...] = total.astype(BF16)


def attn_cotangent(parts, w_held):
    rows, width = parts[0].shape
    return pl.pallas_call(
        d_attn_kernel,
        in_specs=[HELD] * 5,
        out_specs=HELD,
        out_shape=jax.ShapeDtypeStruct((rows, width), BF16),
        compiler_params=pltpu.CompilerParams(vmem_limit_bytes=VMEM_LIMIT),
        cost_estimate=declared(20),
        name="attn_cotangent",
    )(*in_vmem((*parts, w_held)))


def message_kernel(q_ref, attn_ref, d_ref, stat_ref, stat_out, message, sems):
    rows = attn_ref.shape[0]
    copies = [
        pltpu.make_async_copy(ref, message.at[n * rows : (n + 1) * rows], sems.at[n])
        for n, ref in enumerate((q_ref, d_ref))
    ]
    for copy in copies:
        copy.start()
    product = attn_ref[...].astype(F32) * d_ref[...].astype(F32)
    slabs = []
    for g in range(stat_ref.shape[0]):
        stat = stat_ref[g]
        travels = stat
        for i in range(GROUP):
            lo, hi = head_span(i)
            mine = jnp.where(
                head_mask(i, rows, lo, hi), product[:, g * COLS + lo : g * COLS + hi], 0.0
            )
            delta = jnp.sum(mine, axis=1, keepdims=True)
            stat = put_lane(stat, 2 * GROUP + i, delta)
            travels = put_lane(travels, GROUP + i, delta)
        stat_out[g] = stat
        slabs.append(travels.T[: 2 * GROUP])
    rest = jnp.concatenate(slabs, axis=0)
    for n in range(3):
        piece = rest.astype(BF16)
        message[2 * rows :, n * rows : (n + 1) * rows] = piece
        rest = rest - piece.astype(F32)
    for copy in copies:
        copy.wait()


def make_message(q, attn, d_attn, stat):
    rows, width = attn.shape
    return pl.pallas_call(
        message_kernel,
        in_specs=[HELD] * 4,
        out_specs=[HELD] * 2,
        out_shape=[
            jax.ShapeDtypeStruct(stat.shape, F32),
            jax.ShapeDtypeStruct((2 * rows + STAT_ROWS, width), BF16),
        ],
        scratch_shapes=[pltpu.SemaphoreType.DMA((2,))],
        compiler_params=pltpu.CompilerParams(vmem_limit_bytes=VMEM_LIMIT),
        cost_estimate=COST,
        name="message",
    )(*in_vmem((q, attn, d_attn, stat)))


def project_kernel(attn_ref, w_ref, *parts):
    for by, out_ref in zip((1, 3, 2, 0), parts):
        out_ref[...] = dot_nn(attn_ref[...], columns(w_ref, by)).astype(out_ref.dtype)


def project(attn, w_out):
    return pl.pallas_call(
        project_kernel,
        in_specs=[HELD] * 2,
        out_specs=[HELD] * 4,
        out_shape=[jax.ShapeDtypeStruct(attn.shape, BF16)] * 3
        + [jax.ShapeDtypeStruct(attn.shape, F32)],
        compiler_params=pltpu.CompilerParams(vmem_limit_bytes=VMEM_LIMIT),
        cost_estimate=COST,
        name="project",
    )(*in_vmem((attn, w_out)))


def query_grad_kernel(p_ref, d_ref, stat_ref, *refs):
    windows = refs[:BLOCKS]
    out_ref, total = refs[BLOCKS:]
    rows, width = d_ref.shape
    total[...] = jnp.zeros_like(total)
    for h in range(width // HEAD_DIM):
        g, i = h // GROUP, h % GROUP
        lo, hi = head_span(h)
        cot = head_rows(d_ref, h, lo, hi)
        delta = stat_ref[g, :, 2 * GROUP + i : 2 * GROUP + i + 1]
        scale = stat_ref[g, :, GROUP + i : GROUP + i + 1]
        key = jnp.concatenate([w[:rows, lo:hi] for w in windows])
        value = jnp.concatenate([w[rows:, lo:hi] for w in windows])
        d_probs = dot_nt(cot, value)
        d_scores = (p_ref[h].astype(F32) * (d_probs - delta)).astype(BF16)
        add_head(total, h, lo, hi, dot_nn(d_scores, key) * scale)
    out_ref[...] = total[...].astype(BF16)


def query_grad(p, d_attn, stat, windows):
    rows, width = d_attn.shape
    return pl.pallas_call(
        query_grad_kernel,
        in_specs=[HELD] * (3 + len(windows)),
        out_specs=pl.BlockSpec((rows, width), lambda: (0, 0)),
        out_shape=jax.ShapeDtypeStruct((rows, width), BF16),
        scratch_shapes=[pltpu.VMEM((rows, width), F32)],
        compiler_params=pltpu.CompilerParams(vmem_limit_bytes=VMEM_LIMIT),
        cost_estimate=declared(1),
        name="query_grad",
    )(*in_vmem((p, d_attn, stat, *windows)))


def key_grad_kernel(blocks, bias_ref, kv_ref, *refs):
    count = len(blocks)
    messages = refs[:count]
    *so_far, gk_ref, gv_ref, total_k, total_v = refs[count:]
    final = len(so_far) > 2
    if final:
        so_far, out_ref = so_far[:-1], so_far[-1]
        add_parts(*so_far[2:], out_ref)
    rows, width = kv_ref.shape[0] // 2, kv_ref.shape[1]
    half = rows // 2
    stats = []
    for message in messages:
        packed = message[2 * rows :].astype(F32)
        stats.append(packed[:, :rows] + packed[:, rows : 2 * rows] + packed[:, 2 * rows :])
    stats = jnp.concatenate(stats, axis=1)
    bias = jnp.concatenate([bias_ref[:, b * rows : (b + 1) * rows] for b in blocks], axis=1)
    for total, ref in zip((total_k, total_v), so_far[:2] if len(so_far) > 1 else (None, None)):
        total[...] = jnp.zeros_like(total) if ref is None else ref[...]
    for h in range(width // HEAD_DIM):
        lo, hi = head_span(h)
        at_lse = h // GROUP * 2 * GROUP + h % GROUP
        at_delta = at_lse + GROUP
        key = head_rows(kv_ref, h, lo, hi, slice(0, rows))
        value = head_rows(kv_ref, h, lo, hi, slice(rows, 2 * rows))
        query = jnp.concatenate([ref[:rows, lo:hi] for ref in messages])
        cot = jnp.concatenate([ref[rows : 2 * rows, lo:hi] for ref in messages])
        shift = bias - stats[at_lse : at_lse + 1]
        delta = stats[at_delta : at_delta + 1]
        scores = dot_nt(key, query) * (SCALE * LOG2E)
        weights = jnp.exp2(
            jnp.concatenate([scores[:half] + shift[0:1], scores[half:] + shift[1:2]], axis=0)
        )
        grad_v = dot_nn(weights.astype(BF16), cot)
        d_probs = dot_nt(value, cot)
        grad_k = dot_nn((weights * (d_probs - delta)).astype(BF16), query)
        add_head(total_k, h, lo, hi, grad_k)
        add_head(total_v, h, lo, hi, grad_v)
    gk_ref[...] = (total_k[...] * SCALE if final else total_k[...]).astype(gk_ref.dtype)
    gv_ref[...] = total_v[...].astype(gv_ref.dtype)


def add_parts(own, a, b, c, out_ref):
    total = own[...] + a[...].astype(F32) + b[...].astype(F32) + c[...].astype(F32)
    out_ref[...] = total.astype(BF16)


def key_grad(name, blocks, bias, kv, messages, so_far=(), parts=()):
    rows, width = kv.shape[0] // 2, kv.shape[1]
    whole = pl.BlockSpec((rows, width), lambda: (0, 0))
    held = (bias, kv, *messages, *so_far, *parts)
    gives = [whole] * 3 if parts else [HELD] * 2
    return pl.pallas_call(
        partial(key_grad_kernel, blocks),
        in_specs=[HELD] * len(held),
        out_specs=gives,
        out_shape=[jax.ShapeDtypeStruct((rows, width), BF16 if parts else F32)] * len(gives),
        scratch_shapes=[pltpu.VMEM((rows, width), F32)] * 2,
        compiler_params=pltpu.CompilerParams(vmem_limit_bytes=VMEM_LIMIT),
        cost_estimate=COST,
        name=name,
    )(*in_vmem(held))


def gate_kernel(*refs):
    pass


def gate(arrays, after=(), cost=COST):
    return pl.pallas_call(
        gate_kernel,
        in_specs=[ORDER] * (len(arrays) + len(after)),
        out_specs=[ORDER] * len(arrays),
        out_shape=[jax.ShapeDtypeStruct(a.shape, a.dtype) for a in arrays],
        input_output_aliases={n: n for n in range(len(arrays))},
        compiler_params=pltpu.CompilerParams(vmem_limit_bytes=SMALL_LIMIT),
        cost_estimate=cost,
        name="gate",
    )(*in_vmem(arrays), *after)


def pack_kernel(k_ref, v_ref, out_ref, sems):
    rows = k_ref.shape[0]
    copies = [
        pltpu.make_async_copy(ref, out_ref.at[n * rows : (n + 1) * rows], sems.at[n])
        for n, ref in enumerate((k_ref, v_ref))
    ]
    for copy in copies:
        copy.start()
    for copy in copies:
        copy.wait()


def pack(k, v):
    rows, width = k.shape
    return pl.pallas_call(
        pack_kernel,
        in_specs=[ORDER] * 2,
        out_specs=HELD,
        out_shape=jax.ShapeDtypeStruct((2 * rows, width), BF16),
        scratch_shapes=[pltpu.SemaphoreType.DMA((2,))],
        compiler_params=pltpu.CompilerParams(vmem_limit_bytes=SMALL_LIMIT),
        cost_estimate=COST,
        name="pack",
    )(in_hbm(k), in_hbm(v))


def body(queries, keys, values, d_out, w_out, intersection):
    count, length, width = queries.shape
    devices = lax.axis_size("view")
    groups = lax.axis_size("head")
    q, k, v, d = (a.reshape(count * length, width) for a in (queries, keys, values, d_out))

    def from_group(array, by):
        return send(array, "head", [(i, (i - by) % groups) for i in range(groups)])

    gathered = [from_group(d, by) for by in (1, 3, 2)]
    kv = pack(k, v)
    kv_a, kv_b = from_chip_a(kv, devices), from_chip_b(kv, devices)
    w_held, d, q, bias = stage(intersection.T, w_out, d, q)
    (kv_a,) = gate((kv_a,), (w_held,))
    windows = (kv, to_sibling(kv, devices), kv_a, to_sibling(kv_a, devices), kv_b)
    d_attn = attn_cotangent([d] + gathered, w_held)
    attn, p, stat = forward(d_attn, q, bias, windows)
    stat, message = make_message(q, attn, d_attn, stat)
    to_next, to_last, to_far, own = project(attn, w_held)
    d_a, d_b = from_chip_a(message, devices), from_chip_b(message, devices)
    gained = [from_group(part, by) for part, by in ((to_far, 2), (to_next, 3), (to_last, 1))]
    grad_q = query_grad(p, d_attn, stat, windows)
    near = (message, to_sibling(message, devices))
    part = key_grad("key_grad_near", (0, 1), bias, kv, near)
    d_a, d_b = gate((d_a, d_b), (in_hbm(grad_q), part[0]))
    part = key_grad("key_grad_far", (2, 4), bias, kv, (d_a, d_b), part)
    d_last = to_sibling(d_a, devices)
    gained = gate(gained, part[:1], declared(30))
    attended, grad_k, grad_v = key_grad(
        "key_grad_last", (3,), bias, kv, (d_last,), part, (own, *gained)
    )
    shape = (count, length, width)
    return tuple(a.reshape(shape) for a in (attended, grad_q, grad_k, grad_v))


def solution(mesh):
    columns = P("view", None, "head")
    return jax.shard_map(
        body,
        mesh=mesh,
        in_specs=(columns, columns, columns, columns, P("head", None), P()),
        out_specs=(columns, columns, columns, columns),
        check_vma=False,
    )
```
